768 devices in a mesh: dp: 16 (over x, y_hi), pipe: 12 (over z), tensor: 4 (over y_lo, core).
Axes of the slice: x: 4, y: 8 (y_hi: 4, y_lo: 2; y = y_hi * 2 + y_lo), z: 12, core: 2. Of those that a mesh axis runs over, the one named last changes fastest.
Arguments:
- x_stash: bfloat16 [12, 2, 8192, 1536], P('pipe', None, ('dp', 'tensor'))
- h_stash: bfloat16 [12, 2, 8192, 3072], P('pipe', None, 'dp', 'tensor'), may hold values from -8 to 8
- cotangent: bfloat16 [12, 8192, 1536], P('pipe', ('dp', 'tensor')), may hold values from -16 to 16
- plan: int32 [12], P('pipe'), may hold values from 0 to 1, as said below
- conv_w: float32 [12, 7, 1536], P('pipe'), may hold values from -2 to 2
- conv_b: float32 [12, 1536], P('pipe'), may hold values from -5 to 5
- norm_gain: float32 [12, 1536], P('pipe'), may hold values from 0.1 to 1.9
- shift_b: float32 [12, 1536], P('pipe'), may hold values from -3 to 3
- w_in: bfloat16 [12, 1536, 3072], P('pipe', None, 'tensor'), may hold values from -0.15625 to 0.15625
- w_out: bfloat16 [12, 3072, 1536], P('pipe', 'tensor'), may hold values from -0.109375 to 0.109375
Outputs:
- grad_in: bfloat16 [12, 8192, 1536], P('pipe', ('dp', 'tensor'))
- grad_w_in: float32 [12, 1536, 3072], P('pipe', 'dp', 'tensor')
- grad_w_out: float32 [12, 3072, 1536], P('pipe', 'tensor', 'dp')
- grad_conv: float32 [12, 8, 1536], P('pipe')
- grad_affine: float32 [12, 3, 1536], P('pipe')
- grad_b_in: float32 [12, 3072], P('pipe')
The draws below stay inside these ranges and needn't reach their ends.
Inputs may be any that keep to these rules, and one draw needn't show every extreme that they name: `plan`: each of the 2 stashed microbatches is taken by some section.
All inputs are finite; a program needn't handle non-finite values.
Results may differ from the reference program's by a relative error of at most 0.017.
Values may be sent and summed in bfloat16 or wider, within the bound.
A program may use at most 64 MiB of HBM per device.

```python
import math
import jax
import jax.numpy as jnp
from jax import lax

D = 1536
HW = 3072
KER = 7
SLOTS = 2
SEQ = 512
TOKENS = 8192
SEGMENTS = 12
N_DP = 16


def draw_x_stash(key, part):
    subkeys = jax.random.split(key, 3)
    full_shape = (SEGMENTS, SLOTS, TOKENS, D)
    row_scale = jnp.exp(jax.random.uniform(subkeys[1], (SEGMENTS, SLOTS, TOKENS, 1), jnp.float32, 0.0, math.log(10.0)))
    col_scale = jnp.exp(jax.random.uniform(subkeys[2], (1, 1, 1, D), jnp.float32, 0.0, math.log(3.0)))
    base_draw = jax.random.normal(subkeys[0], full_shape, jnp.float32)
    return (0.25 * base_draw * row_scale * col_scale).astype(jnp.bfloat16)


def draw_plan(key, part):
    cyclic = jnp.arange(SEGMENTS, dtype=jnp.int32) % SLOTS
    return jax.random.permutation(key, cyclic).astype(jnp.int32)


def raised(entries, own_key, source, target, parts, factor):
    owner, partner = [(jnp.arange(entries.shape[axis_at]) // (entries.shape[axis_at] // parts)).reshape([-1 if axis == axis_at else 1 for axis in range(entries.ndim)]) for axis_at in (source, target)]
    chosen = jax.random.permutation(own_key, parts)[partner]
    strong = (owner == chosen) | (owner == (partner + parts // 2) % parts)
    return jnp.where(strong, factor * entries, entries)


def block_scale(own_key, dims, cuts, low, largest):
    def one(dim, shards_of):
        steps = jax.random.uniform(jax.random.fold_in(jax.random.fold_in(own_key, 6), dim), (shards_of,), jnp.float32, low / len(cuts), largest / len(cuts))
        return jnp.repeat(jnp.exp(steps), dims[dim] // shards_of).reshape((-1,) + (1,) * (len(dims) - dim - 1))

    loudness = one(*cuts[0])
    for cut in cuts[1:]:
        loudness = loudness * one(*cut)
    return loudness


def normal_values(stream_key, dims, spread, bound, cuts=(), kind=jnp.bfloat16):
    drawn = spread * jax.random.normal(stream_key, dims, jnp.float32)
    if cuts:
        drawn = drawn * block_scale(stream_key, dims, cuts, -0.22, 0.18)
    return jnp.clip(drawn, -bound, bound).astype(kind)


def gaussian_with(key, shape, spread, bound, cuts, heavy, held_as=jnp.bfloat16):
    entries = spread * jax.random.normal(key, shape, jnp.float32)
    if cuts:
        entries = entries * block_scale(key, shape, cuts, -0.22, 0.18)
    return jnp.clip(raised(entries, jax.random.fold_in(key, 3), *heavy), -bound, bound).astype(held_as)


def setup_inputs(seed: int = 0) -> dict:
    splits = jax.random.split(jax.random.key(seed), 11)
    return {
        "x_stash": draw_x_stash(jax.random.fold_in(splits[10], 71), 0),
        "h_stash": normal_values(splits[1], (SEGMENTS, SLOTS, TOKENS, HW), 1.5, 8.0, ((0, 12), (2, 16), (3, 4))),
        "cotangent": gaussian_with(splits[2], (SEGMENTS, TOKENS, D), 1.0, 16.0, ((0, 12), (1, 64)), (1, 2, 64, 4.0)),
        "plan": draw_plan(jax.random.fold_in(splits[10], 71), 0),
        "conv_w": normal_values(splits[4], (SEGMENTS, KER, D), KER ** -0.5, 2.0, ((0, 12),), jnp.float32),
        "conv_b": normal_values(splits[5], (SEGMENTS, D), 1.0, 5.0, ((0, 12),), jnp.float32),
        "norm_gain": jnp.clip(1.0 + 0.18 * jax.random.normal(splits[6], (SEGMENTS, D), jnp.float32), 0.1, 1.9),
        "shift_b": normal_values(splits[7], (SEGMENTS, D), 0.5, 3.0, ((0, 12),), jnp.float32),
        "w_in": normal_values(splits[8], (SEGMENTS, D, HW), D ** -0.5, 0.15625, ((0, 12), (2, 4))),
        "w_out": normal_values(splits[9], (SEGMENTS, HW, D), HW ** -0.5, 0.109375, ((0, 12), (1, 4))),
    }


gelu_coef = 0.044715
root_coef = math.sqrt(2.0 / math.pi)
norm_eps = 1e-06

def gelu_pair(hidden):
    inner_arg = root_coef * (hidden + gelu_coef * hidden * hidden * hidden)
    tangent = jnp.tanh(inner_arg)
    gelu_value = 0.5 * hidden * (1.0 + tangent)
    gelu_slope = 0.5 * (1.0 + tangent) + 0.5 * hidden * (1.0 - tangent * tangent) * root_coef * (1.0 + 3.0 * gelu_coef * hidden * hidden)
    return (gelu_value, gelu_slope)

def forward_norm(x_seq, kernel_w, kernel_b, gain_v, shift_v):
    kernel = kernel_w.shape[0]
    margin = kernel // 2
    length = x_seq.shape[0]
    padded = jnp.pad(x_seq.astype(jnp.float32), ((margin, margin), (0, 0)))
    conv_out = kernel_b + sum((kernel_w[kernel_tap] * padded[kernel_tap:kernel_tap + length] for kernel_tap in range(kernel)))
    center = conv_out - lax.optimization_barrier(jnp.mean(conv_out, -1, keepdims=True))
    inv_std = lax.rsqrt(lax.optimization_barrier(jnp.mean(center * center, -1, keepdims=True)) + norm_eps)
    normed = center * inv_std
    scaled = (normed * gain_v + shift_v).astype(jnp.bfloat16)
    return (padded, normed, inv_std, scaled)

def block_grad(x_seq, h_seq, g_seq, kernel_w, kernel_b, gain_v, shift_v, weight_in, weight_out):
    kernel = kernel_w.shape[0]
    margin = kernel // 2
    length = x_seq.shape[0]
    padded, normed, inv_std, scaled = forward_norm(x_seq, kernel_w, kernel_b, gain_v, shift_v)
    gelu_value, gelu_slope = gelu_pair(h_seq.astype(jnp.float32))
    active = gelu_value.astype(jnp.bfloat16)
    d_act = jnp.dot(g_seq, weight_out.T, preferred_element_type=jnp.float32)
    d_hidden = d_act * gelu_slope
    d_hidden_b = d_hidden.astype(jnp.bfloat16)
    grad_win = jnp.dot(scaled.T, d_hidden_b, preferred_element_type=jnp.float32)
    grad_wout_t = jnp.dot(g_seq.T, active, preferred_element_type=jnp.float32)
    grad_bin = lax.optimization_barrier(jnp.sum(d_hidden, 0))
    d_scaled = jnp.dot(d_hidden_b, weight_in.T, preferred_element_type=jnp.float32)
    grad_gain = lax.optimization_barrier(jnp.sum(d_scaled * normed, 0))
    grad_shift = lax.optimization_barrier(jnp.sum(d_scaled, 0))
    d_normed = d_scaled * gain_v
    d_mixed = inv_std * (d_normed - lax.optimization_barrier(jnp.mean(d_normed, -1, keepdims=True)) - normed * lax.optimization_barrier(jnp.mean(d_normed * normed, -1, keepdims=True)))
    grad_convb = lax.optimization_barrier(jnp.sum(d_mixed, 0))
    grad_convw = jnp.stack([lax.optimization_barrier(jnp.sum(d_mixed * padded[kernel_tap:kernel_tap + length], 0)) for kernel_tap in range(kernel)])
    d_padded = jnp.pad(d_mixed, ((margin, margin), (0, 0)))
    d_input = sum((kernel_w[kernel_tap] * d_padded[2 * margin - kernel_tap:2 * margin - kernel_tap + length] for kernel_tap in range(kernel)))
    grad_x = (g_seq.astype(jnp.float32) + d_input).astype(jnp.bfloat16)
    grad_bout = lax.optimization_barrier(jnp.sum(g_seq.astype(jnp.float32), 0))
    conv_grad = jnp.concatenate([grad_convw, grad_convb[None]], 0)
    affine_grad = jnp.stack([grad_gain, grad_shift, grad_bout])
    return (grad_win, grad_wout_t, conv_grad, affine_grad, grad_bin, grad_x)

def reference(x_stash, h_stash, cotangent, plan, conv_w, conv_b, norm_gain, shift_b, w_in, w_out):

    def one_segment(segment_index):
        stash_slot = plan[segment_index]
        x_all = x_stash[segment_index, stash_slot].reshape(N_DP, SEQ, D)
        h_all = h_stash[segment_index, stash_slot].reshape(N_DP, SEQ, HW)
        g_all = cotangent[segment_index].reshape(N_DP, SEQ, D)
        kernel_w = conv_w[segment_index]
        kernel_b = conv_b[segment_index]
        gain_v = norm_gain[segment_index]
        shift_v = shift_b[segment_index]
        weight_in = w_in[segment_index]
        weight_out = w_out[segment_index]

        def replica(totals, pieces):
            grad_win, grad_wout_t, conv_grad, affine_grad, grad_bin, grad_x = block_grad(pieces[0], pieces[1], pieces[2], kernel_w, kernel_b, gain_v, shift_v, weight_in, weight_out)
            rounded_in = lax.optimization_barrier(grad_win.astype(jnp.bfloat16)).astype(jnp.float32)
            rounded_out = lax.optimization_barrier(grad_wout_t.astype(jnp.bfloat16)).astype(jnp.float32)
            totals = (totals[0] + rounded_in, totals[1] + rounded_out, totals[2] + conv_grad, totals[3] + affine_grad, totals[4] + grad_bin)
            return (totals, grad_x)
        initial = (jnp.zeros((D, HW), jnp.float32), jnp.zeros((D, HW), jnp.float32), jnp.zeros((KER + 1, D), jnp.float32), jnp.zeros((3, D), jnp.float32), jnp.zeros((HW,), jnp.float32))
        totals, segment_grads = lax.scan(replica, initial, (x_all, h_all, g_all))
        return (totals[0], totals[1].T, totals[2], totals[3], totals[4], segment_grads.reshape(TOKENS, D))
    results = lax.map(one_segment, jnp.arange(SEGMENTS, dtype=jnp.int32))
    grad_in = jnp.concatenate([results[5][1:], jnp.zeros_like(results[5][:1])], 0)
    return (grad_in, results[0], results[1], results[2], results[3], results[4])
```

```python
import math

import jax
import jax.numpy as jnp
from jax import lax
from jax.experimental import pallas as pl
from jax.experimental.pallas import tpu as pltpu
from jax.sharding import PartitionSpec as P

MESH = pl.DeviceIdType.MESH
f32 = jnp.float32
bf16 = jnp.bfloat16

gelu_coef = 0.044715
root_coef = math.sqrt(2.0 / math.pi)
norm_eps = 1e-06

D = 1536
HID = 768
SEQ = 512
TOK = 128
KER = 7
CH = 384
XB = D // 4
YB = XB // 4
WIDE = TOK + 16
N_COPIES = 96
N_LOCAL = 16


def dot_tn(a, b):
    return lax.dot_general(a, b, (((0,), (0,)), ((), ())), preferred_element_type=f32)


def dot_nt(a, b):
    return lax.dot_general(a, b, (((1,), (1,)), ((), ())), preferred_element_type=f32)


def kernel(
    x_hbm, h_hbm, g_hbm, plan_ref, cw_ref, cb_ref, gain_ref, shift_ref, win_hbm, wout_hbm,
    gin_out, gwi_out, gwo_out, small_out,
    xs, hs, gf, sf, win, wout, halo, xw, normed, inv, active, slope, dh, dpart, s1, r1, s2, r2t,
    part, xr2, xrx, q, yr2, yrx, dmix, gx, accs, sm, arc, ar, arr, bias, ssem, rsem, lsem,
):
    dp = lax.axis_index("dp")
    pz = lax.axis_index("pipe")
    t = lax.axis_index("tensor")
    xi, yi = dp // 4, dp % 4
    ylo, core = t // 2, t % 2
    npipe = lax.axis_size("pipe")

    def dev(dp_=None, pz_=None, t_=None):
        return (
            dp if dp_ is None else dp_,
            pz if pz_ is None else pz_,
            t if t_ is None else t_,
        )

    core_dev = dev(t_=ylo * 2 + 1 - core)
    chip_dev = dev(t_=(t + 2) % 4)
    diag_dev = dev(t_=(1 - ylo) * 2 + 1 - core)
    seq_next, seq_prev = dev(t_=(t + 1) % 4), dev(t_=(t + 3) % 4)
    xp, xm = dev(dp_=((xi + 1) % 4) * 4 + yi), dev(dp_=((xi + 3) % 4) * 4 + yi)
    yp, ym = dev(dp_=xi * 4 + (yi + 1) % 4), dev(dp_=xi * 4 + (yi + 3) % 4)
    x_a = dev(dp_=(xi + 1 - 2 * (xi % 2)) * 4 + yi)
    x_b = dev(dp_=(3 - xi) * 4 + yi)
    y_a = dev(dp_=xi * 4 + yi + 1 - 2 * (yi % 2))
    y_b = dev(dp_=xi * 4 + 3 - yi)
    z_down = dev(pz_=(pz + npipe - 1) % npipe)
    z_up = dev(pz_=(pz + 1) % npipe)

    used = [0, 0]
    sent = []

    def remote(src, dst, to):
        i = used[0]
        used[0] += 1
        assert i < N_COPIES
        copy = pltpu.make_async_remote_copy(
            src_ref=src, dst_ref=dst, send_sem=ssem.at[i], recv_sem=rsem.at[i],
            device_id=to, device_id_type=MESH,
        )
        copy.start()
        sent.append(copy)
        return copy

    def local(src, dst):
        i = used[1]
        used[1] += 1
        assert i < N_LOCAL
        copy = pltpu.make_async_copy(src, dst, lsem.at[i])
        copy.start()
        return copy

    own_rows = pl.ds(pl.multiple_of(t * TOK, TOK), TOK)

    lx = local(x_hbm.at[0], xs)
    lh = local(h_hbm.at[0], hs)
    lg = local(g_hbm.at[0], gf.at[own_rows])
    lwo = local(wout_hbm.at[0], wout)
    lwi = local(win_hbm.at[0], win)

    barrier = pltpu.get_barrier_semaphore()
    for to in (core_dev, chip_dev, diag_dev, xp, xm, yp, ym, z_down, z_up):
        pl.semaphore_signal(barrier, inc=1, device_id=to, device_id_type=MESH)
    pl.semaphore_wait(barrier, 9)

    g_chip = remote(g_hbm.at[0], gf.at[own_rows], chip_dev)
    slot = plan_ref[0]
    lx.wait()
    halo[0] = xs[slot, TOK - 16 :, :]
    halo[1] = xs[slot, :16, :]
    h_next = remote(halo.at[0], halo.at[2], seq_next)
    h_prev = remote(halo.at[1], halo.at[3], seq_prev)
    g_core = remote(g_hbm.at[0], gf.at[own_rows], core_dev)

    def widen(i, carry):
        rows = pl.ds(pl.multiple_of(i * 16, 16), 16)
        xw[pl.ds(pl.multiple_of(16 + i * 16, 16), 16), :] = xs[slot, rows, :].astype(f32)
        return carry

    lax.fori_loop(0, TOK // 16, widen, 0)

    lh.wait()

    def gelu_rows(i, carry):
        rows = pl.ds(pl.multiple_of(i * 16, 16), 16)
        hv = hs[slot, rows, :].astype(f32)
        square = hv * hv
        tangent = jnp.tanh(root_coef * hv * (1.0 + gelu_coef * square))
        half = 0.5 + 0.5 * tangent
        value = hv * half
        active[rows, :] = value.astype(bf16)
        slope[rows, :] = half + value * (1.0 - tangent) * (
            root_coef + (3.0 * gelu_coef * root_coef) * square
        )
        return carry

    lax.fori_loop(0, SEQ // 16, gelu_rows, 0)

    h_next.wait_recv()
    h_prev.wait_recv()
    xw[0:16, :] = jnp.where(t > 0, halo[2].astype(f32), 0.0)
    xw[16 + TOK : 32 + TOK, :] = jnp.where(t < 3, halo[3].astype(f32), 0.0)

    def norm_rows(first, count):
        near = xw[pl.ds(first, count + 16), :]
        out = cb_ref[...] + cw_ref[0:1, :] * near[5 : 5 + count]
        for k in range(1, KER):
            out = out + cw_ref[k : k + 1, :] * near[5 + k : 5 + k + count]
        center = out - jnp.mean(out, -1, keepdims=True)
        istd = lax.rsqrt(jnp.mean(center * center, -1, keepdims=True) + norm_eps)
        return center * istd, istd

    def own_norm(i, carry):
        rows = pl.ds(pl.multiple_of(i * 16, 16), 16)
        value, istd = norm_rows(pl.multiple_of(16 * i + 8, 8), 16)
        normed[rows, :] = value
        inv[rows, :] = jnp.broadcast_to(istd, (16, 128))
        sf[pl.ds(pl.multiple_of(t * TOK + i * 16, 16), 16), :] = (
            value * gain_ref[...] + shift_ref[...]
        ).astype(bf16)
        return carry

    lax.fori_loop(0, TOK // 16, own_norm, 0)
    s_chip = remote(sf.at[own_rows], sf.at[own_rows], chip_dev)
    s_core = remote(sf.at[own_rows], sf.at[own_rows], core_dev)
    for first, row in ((0, TOK), (TOK + 8, TOK + 8)):
        value, istd = norm_rows(first, 8)
        normed[row : row + 8, :] = value
        inv[row : row + 8, :] = jnp.broadcast_to(istd, (8, 128))

    def hidden_grads(half):
        base = pl.multiple_of(half * 256, 256)
        for j in range(2):
            cols = pl.ds(j * CH, CH)
            d = dot_nt(gf[pl.ds(base, 256), :], wout[j * CH : (j + 1) * CH, :])
            d = d * slope[pl.ds(base, 256), cols]
            bias[:, cols] += jnp.sum(d, 0, keepdims=True)
            dh[pl.ds(base, 256), cols] = d.astype(bf16)

    def part_scaled(half):
        base = pl.multiple_of(half * 256, 256)

        def block(j, carry):
            cols = pl.ds(pl.multiple_of(j * CH, CH), CH)
            dpart[pl.ds(pl.multiple_of(base + 8, 8), 256), cols] = dot_nt(
                dh[pl.ds(base, 256), :], win[cols, :]
            )
            return carry

        lax.fori_loop(0, D // CH, block, 0)

    bias[...] = jnp.zeros_like(bias)
    dpart[0:8, :] = jnp.zeros((8, D), f32)
    dpart[SEQ + 8 : SEQ + 16, :] = jnp.zeros((8, D), f32)
    lwo.wait()
    lg.wait()
    g_core.wait_recv()
    hidden_grads(ylo)
    lwi.wait()
    part_scaled(ylo)

    g_chip.wait_recv()
    chip_rows = pl.ds(pl.multiple_of(((t + 2) % 4) * TOK, TOK), TOK)
    g_pass = remote(gf.at[chip_rows], gf.at[chip_rows], core_dev)
    g_pass.wait_recv()

    def weight_part(c, src, hidden):
        cols = pl.ds((c % 2) * CH, CH)

        def block(k, carry):
            target = pl.multiple_of(((xi + k) % 4) * XB, XB)
            part[c, k] = dot_tn(src[:, pl.ds(target, XB)], hidden[:, cols]).astype(bf16)
            return carry

        lax.fori_loop(0, 4, block, 0)

    def ring_first(own, two, last, half, plus, minus):
        far_a = remote(own.at[2, pl.ds(0, half)], two.at[0], plus)
        far_b = remote(own.at[2, pl.ds(half, half)], two.at[1], minus)
        near_b = remote(own.at[1, pl.ds(half, half)], last.at[0, pl.ds(half, half)], plus)
        near_a = remote(own.at[3, pl.ds(0, half)], last.at[1, pl.ds(0, half)], minus)
        return far_a, far_b, near_a, near_b

    def ring_second(copies, own, two, last, half, plus, minus):
        far_a, far_b, near_a, near_b = copies
        far_a.wait_recv()

        def add_a(i, carry):
            rows = pl.ds(pl.multiple_of(i * 48, 16), 48)
            own[1, rows, :] = (own[1, rows, :].astype(f32) + two[0, rows, :].astype(f32)).astype(bf16)
            return carry

        lax.fori_loop(0, half // 48, add_a, 0)
        sum_a = remote(own.at[1, pl.ds(0, half)], last.at[0, pl.ds(0, half)], plus)
        far_b.wait_recv()

        def add_b(i, carry):
            rows = pl.ds(pl.multiple_of(half + i * 48, 16), 48)
            here = pl.ds(pl.multiple_of(i * 48, 16), 48)
            own[3, rows, :] = (own[3, rows, :].astype(f32) + two[1, here, :].astype(f32)).astype(bf16)
            return carry

        lax.fori_loop(0, half // 48, add_b, 0)
        sum_b = remote(own.at[3, pl.ds(half, half)], last.at[1, pl.ds(half, half)], minus)
        return near_a, near_b, sum_a, sum_b

    x_copies, y_copies = {}, {}

    def x_first(c):
        x_copies[c] = ring_first(part.at[c], xr2.at[c], xrx.at[c], XB // 2, xp, xm)

    def x_second(c):
        x_copies[c] = ring_second(x_copies[c], part.at[c], xr2.at[c], xrx.at[c], XB // 2, xp, xm)

    def x_third(c):
        for copy in x_copies[c]:
            copy.wait_recv()

        def block(k, carry):
            for piece in range(2):
                rows = pl.ds(pl.multiple_of(((yi + k) % 4) * YB + piece * 48, 16), 48)
                q[c, k, pl.ds(piece * 48, 48), :] = (
                    part[c, 0, rows, :].astype(f32)
                    + xrx[c, 0, rows, :].astype(f32)
                    + xrx[c, 1, rows, :].astype(f32)
                ).astype(bf16)
            return carry

        lax.fori_loop(0, 4, block, 0)

    def y_first(c):
        y_copies[c] = ring_first(q.at[c], yr2.at[c], yrx.at[c], YB // 2, yp, ym)

    def y_second(c):
        y_copies[c] = ring_second(y_copies[c], q.at[c], yr2.at[c], yrx.at[c], YB // 2, yp, ym)

    def y_third(c):
        for copy in y_copies[c]:
            copy.wait_recv()
        out = gwo_out if c < 2 else gwi_out
        for piece in range(2):
            rows = pl.ds(piece * 48, 48)
            out[rows, pl.ds((c % 2) * CH, CH)] = (
                q[c, 0, rows, :].astype(f32)
                + yrx[c, 0, rows, :].astype(f32)
                + yrx[c, 1, rows, :].astype(f32)
            )

    weight_part(0, gf, active)
    x_first(0)

    hidden_grads(1 - ylo)
    part_scaled(1 - ylo)

    def target_rows(tt, i):
        return dpart[pl.ds(pl.multiple_of(8 + tt * TOK + i * 16, 8), 16), :]

    def target_rim(tt, after):
        return dpart[pl.ds(pl.multiple_of(tt * TOK + after * (TOK + 8), 8), 8), :]

    core_far = (1 - ylo) * 2 + 1 - core
    core_near = ylo * 2 + 1 - core
    core_sums = []
    for n, tt in enumerate((core_far, core_near)):

        def fill(i, carry, n=n, tt=tt):
            s1[n, pl.ds(pl.multiple_of(i * 16, 16), 16), :] = target_rows(tt, i).astype(bf16)
            return carry

        lax.fori_loop(0, TOK // 16, fill, 0)
        s1[n, TOK:, :] = jnp.concatenate([target_rim(tt, 0), target_rim(tt, 1)], 0).astype(bf16)
        core_sums.append(remote(s1.at[n], r1.at[n], core_dev))

    weight_part(1, gf, active)
    x_first(1)

    core_sums[0].wait_recv()
    chip_t = (t + 2) % 4

    def add_far(i, carry):
        rows = pl.ds(pl.multiple_of(i * 16, 16), 16)
        s2[rows, :] = (target_rows(chip_t, i) + r1[0, rows, :].astype(f32)).astype(bf16)
        return carry

    lax.fori_loop(0, TOK // 16, add_far, 0)
    s2[TOK:, :] = (
        jnp.concatenate([target_rim(chip_t, 0), target_rim(chip_t, 1)], 0) + r1[0, TOK:, :].astype(f32)
    ).astype(bf16)
    far_sum = remote(s2, r2t, chip_dev)

    x_second(0)

    s_chip.wait_recv()
    s_pass = remote(sf.at[chip_rows], sf.at[chip_rows], core_dev)
    s_core.wait_recv()
    s_pass.wait_recv()
    weight_part(2, sf, dh)
    x_first(2)
    x_second(1)
    weight_part(3, sf, dh)
    x_third(0)
    y_first(0)

    core_sums[1].wait_recv()
    far_sum.wait_recv()
    accs[...] = jnp.zeros_like(accs)

    def norm_back(ds, rows, count):
        nv = normed[rows, :]
        dn = ds * gain_ref[...]
        mean_d = jnp.mean(dn, -1, keepdims=True)
        mean_p = jnp.mean(dn * nv, -1, keepdims=True)
        return nv, inv[rows, 0:1] * (dn - mean_d - nv * mean_p)

    def own_back(i, carry):
        rows = pl.ds(pl.multiple_of(i * 16, 16), 16)
        ds = target_rows(t, i) + r1[1, rows, :].astype(f32) + r2t[rows, :].astype(f32)
        nv, dm = norm_back(ds, rows, 16)
        dmix[pl.ds(pl.multiple_of(8 + i * 16, 8), 16), :] = dm
        dsn = ds * nv
        accs[0] += dsn[0:8] + dsn[8:16]
        accs[1] += ds[0:8] + ds[8:16]
        return carry

    lax.fori_loop(0, TOK // 16, own_back, 0)
    rim = pl.ds(TOK, 16)
    rim_ds = (
        jnp.concatenate([target_rim(t, 0), target_rim(t, 1)], 0)
        + r1[1, TOK:, :].astype(f32)
        + r2t[TOK:, :].astype(f32)
    )
    _, rim_dm = norm_back(rim_ds, rim, 16)
    dmix[0:8, :] = rim_dm[0:8]
    dmix[TOK + 8 : TOK + 16, :] = rim_dm[8:16]


    def input_rows(i, carry):
        near = dmix[pl.ds(pl.multiple_of(16 * i, 16), 32), :]
        d = cw_ref[0:1, :] * near[11:27]
        for k in range(1, KER):
            d = d + cw_ref[k : k + 1, :] * near[11 - k : 27 - k]
        gv = gf[pl.ds(pl.multiple_of(t * TOK + i * 16, 16), 16), :].astype(f32)
        gx[pl.ds(pl.multiple_of(i * 16, 16), 16), :] = jnp.where(pz > 0, gv + d, 0.0).astype(bf16)
        return carry

    z_copies = []
    for piece in range(2):
        lax.fori_loop(piece * 4, piece * 4 + 4, input_rows, 0)
        rows = pl.ds(piece * 64, 64)
        z_copies.append(remote(gx.at[rows], gin_out.at[0, rows], z_down))

    x_first(3)

    sm[...] = jnp.zeros_like(sm)

    def tap_sums(j, carry):
        cols = pl.ds(pl.multiple_of(j * 256, 256), 256)

        def rows_step(i, totals):
            dm = dmix[pl.ds(pl.multiple_of(8 + 8 * i, 8), 8), cols]
            near = xw[pl.ds(pl.multiple_of(8 + 8 * i, 8), 24), cols]
            out = [totals[k] + dm * near[5 + k : 13 + k] for k in range(KER)]
            out.append(totals[KER] + dm)
            return tuple(out)

        totals = lax.fori_loop(
            0, TOK // 8, rows_step, tuple(jnp.zeros((8, 256), f32) for _ in range(KER + 1))
        )
        for k in range(KER + 1):
            sm[k : k + 1, cols] = jnp.sum(totals[k], 0, keepdims=True)

        def g_step(i, total):
            gv = gf[pl.ds(pl.multiple_of(t * TOK + i * 16, 16), 16), cols].astype(f32)
            return total + gv[0:8] + gv[8:16]

        total = lax.fori_loop(0, TOK // 16, g_step, jnp.zeros((8, 256), f32))
        sm[10:11, cols] = jnp.sum(total, 0, keepdims=True)
        sm[8:9, cols] = jnp.sum(accs[0, :, cols], 0, keepdims=True)
        sm[9:10, cols] = jnp.sum(accs[1, :, cols], 0, keepdims=True)
        return carry

    lax.fori_loop(0, D // 256, tap_sums, 0)
    zero_row = jnp.zeros((1, HID), f32)
    for s in range(4):
        sm[11 + s // 2 : 12 + s // 2, (s % 2) * HID : (s % 2 + 1) * HID] = jnp.where(
            t == s, bias[...], zero_row
        )
    a_core = remote(sm, arc, core_dev)

    x_second(2)

    a_core.wait_recv()
    my8 = pl.ds(pl.multiple_of(core * 8, 8), 8)
    ar[0] = sm[my8, :] + arc[my8, :]
    partners = (chip_dev, x_a, x_b, y_a, y_b)
    a_copy = remote(ar.at[0], arr.at[0], partners[0])

    def a_step(n):
        a_copy.wait_recv()
        ar[n] = ar[n - 1] + arr[n - 1]
        if n < len(partners):
            return remote(ar.at[n], arr.at[n], partners[n])
        return None

    x_third(1)
    y_first(1)
    a_copy = a_step(1)
    y_second(0)
    y_third(0)
    a_copy = a_step(2)
    x_second(3)
    a_copy = a_step(3)
    x_third(2)
    y_first(2)
    a_copy = a_step(4)
    y_second(1)
    y_third(1)
    a_step(5)
    small_out[my8, :] = ar[5]
    a_back = remote(ar.at[5], small_out.at[my8], core_dev)
    y_second(2)
    x_third(3)
    y_first(3)
    y_third(2)
    y_second(3)
    y_third(3)
    a_back.wait_recv()
    for copy in z_copies:
        copy.wait_recv()
    for copy in sent:
        copy.wait_send()


def per_device(x_stash, h_stash, cotangent, plan, conv_w, conv_b, norm_gain, shift_b, w_in, w_out):
    anyspace = pl.BlockSpec(memory_space=pl.ANY)
    vmem = pl.BlockSpec(memory_space=pltpu.VMEM)
    smem = pl.BlockSpec(memory_space=pltpu.SMEM)
    gin, gwi, gwo, small = pl.pallas_call(
        kernel,
        out_shape=(
            jax.ShapeDtypeStruct((1, TOK, D), bf16),
            jax.ShapeDtypeStruct((YB, HID), f32),
            jax.ShapeDtypeStruct((YB, HID), f32),
            jax.ShapeDtypeStruct((16, D), f32),
        ),
        in_specs=[anyspace, anyspace, anyspace, smem, vmem, vmem, vmem, vmem, anyspace, anyspace],
        out_specs=(anyspace, vmem, vmem, vmem),
        scratch_shapes=[
            pltpu.VMEM((2, TOK, D), bf16),
            pltpu.VMEM((2, SEQ, HID), bf16),
            pltpu.VMEM((SEQ, D), bf16),
            pltpu.VMEM((SEQ, D), bf16),
            pltpu.VMEM((D, HID), bf16),
            pltpu.VMEM((HID, D), bf16),
            pltpu.VMEM((4, 16, D), bf16),
            pltpu.VMEM((TOK + 32, D), f32),
            pltpu.VMEM((WIDE, D), f32),
            pltpu.VMEM((WIDE, 128), f32),
            pltpu.VMEM((SEQ, HID), bf16),
            pltpu.VMEM((SEQ, HID), f32),
            pltpu.VMEM((SEQ, HID), bf16),
            pltpu.VMEM((SEQ + 16, D), f32),
            pltpu.VMEM((2, WIDE, D), bf16),
            pltpu.VMEM((2, WIDE, D), bf16),
            pltpu.VMEM((WIDE, D), bf16),
            pltpu.VMEM((WIDE, D), bf16),
            pltpu.VMEM((4, 4, XB, CH), bf16),
            pltpu.VMEM((4, 2, XB // 2, CH), bf16),
            pltpu.VMEM((4, 2, XB, CH), bf16),
            pltpu.VMEM((4, 4, YB, CH), bf16),
            pltpu.VMEM((4, 2, YB // 2, CH), bf16),
            pltpu.VMEM((4, 2, YB, CH), bf16),
            pltpu.VMEM((WIDE, D), f32),
            pltpu.VMEM((TOK, D), bf16),
            pltpu.VMEM((2, 8, D), f32),
            pltpu.VMEM((16, D), f32),
            pltpu.VMEM((16, D), f32),
            pltpu.VMEM((6, 8, D), f32),
            pltpu.VMEM((5, 8, D), f32),
            pltpu.VMEM((1, HID), f32),
            pltpu.SemaphoreType.DMA((N_COPIES,)),
            pltpu.SemaphoreType.DMA((N_COPIES,)),
            pltpu.SemaphoreType.DMA((N_LOCAL,)),
        ],
        compiler_params=pltpu.CompilerParams(
            collective_id=0, has_side_effects=True, vmem_limit_bytes=56 * 1024 * 1024
        ),
    )(
        x_stash, h_stash, cotangent, plan, conv_w[0], conv_b, norm_gain, shift_b, w_in, w_out
    )
    return (
        gin,
        gwi[None],
        gwo.T[None],
        small[None, 0:8],
        small[None, 8:11],
        small[11:13].reshape(1, 2 * D),
    )


def solution(mesh):
    return jax.shard_map(
        per_device,
        mesh=mesh,
        in_specs=(
            P("pipe", None, ("dp", "tensor"), None),
            P("pipe", None, "dp", "tensor"),
            P("pipe", ("dp", "tensor"), None),
            P("pipe"),
            P("pipe", None, None),
            P("pipe", None),
            P("pipe", None),
            P("pipe", None),
            P("pipe", None, "tensor"),
            P("pipe", "tensor", None),
        ),
        out_specs=(
            P("pipe", ("dp", "tensor"), None),
            P("pipe", "dp", "tensor"),
            P("pipe", "tensor", "dp"),
            P("pipe", None, None),
            P("pipe", None, None),
            P("pipe", None),
        ),
        check_vma=False,
    )
```

```python
import math

import jax
import jax.numpy as jnp
from jax import lax
from jax.experimental import pallas as pl
from jax.experimental.pallas import tpu as pltpu
from jax.sharding import PartitionSpec as P

MESH = pl.DeviceIdType.MESH
f32 = jnp.float32
bf16 = jnp.bfloat16

gelu_coef = 0.044715
root_coef = math.sqrt(2.0 / math.pi)
norm_eps = 1e-06

D = 1536
HID = 768
SEQ = 512
TOK = 128
KER = 7
CH = 384
XB = D // 4
YB = XB // 4
WIDE = TOK + 16
N_COPIES = 112
N_LOCAL = 16


def dot_tn(a, b):
    return lax.dot_general(a, b, (((0,), (0,)), ((), ())), preferred_element_type=f32)


def dot_nt(a, b):
    return lax.dot_general(a, b, (((1,), (1,)), ((), ())), preferred_element_type=f32)


def kernel(
    x_hbm, h_hbm, g_hbm, plan_ref, cw_ref, cb_ref, gain_ref, shift_ref, win_hbm, wout_hbm,
    gin_out, gwi_out, gwo_out, small_out,
    xs, hs, gf, sf, win, wout, halo, xw, normed, inv, active, slope, dh, dpart, s1, r1, s2, r2t,
    part, xr2, xrx, q, yr2, yrx, dmix, gx, accs, sm, arc, ar, arr, bias, ssem, rsem, lsem,
):
    dp = lax.axis_index("dp")
    pz = lax.axis_index("pipe")
    t = lax.axis_index("tensor")
    xi, yi = dp // 4, dp % 4
    ylo, core = t // 2, t % 2
    npipe = lax.axis_size("pipe")

    def dev(dp_=None, pz_=None, t_=None):
        return (
            dp if dp_ is None else dp_,
            pz if pz_ is None else pz_,
            t if t_ is None else t_,
        )

    core_dev = dev(t_=ylo * 2 + 1 - core)
    chip_dev = dev(t_=(t + 2) % 4)
    diag_dev = dev(t_=(1 - ylo) * 2 + 1 - core)
    seq_next, seq_prev = dev(t_=(t + 1) % 4), dev(t_=(t + 3) % 4)
    xp, xm = dev(dp_=((xi + 1) % 4) * 4 + yi), dev(dp_=((xi + 3) % 4) * 4 + yi)
    yp, ym = dev(dp_=xi * 4 + (yi + 1) % 4), dev(dp_=xi * 4 + (yi + 3) % 4)
    x_a = dev(dp_=(xi + 1 - 2 * (xi % 2)) * 4 + yi)
    x_b = dev(dp_=(3 - xi) * 4 + yi)
    y_a = dev(dp_=xi * 4 + yi + 1 - 2 * (yi % 2))
    y_b = dev(dp_=xi * 4 + 3 - yi)
    z_down = dev(pz_=(pz + npipe - 1) % npipe)
    z_up = dev(pz_=(pz + 1) % npipe)

    used = [0, 0]
    sent = []

    def remote(src, dst, to):
        i = used[0]
        used[0] += 1
        assert i < N_COPIES
        copy = pltpu.make_async_remote_copy(
            src_ref=src, dst_ref=dst, send_sem=ssem.at[i], recv_sem=rsem.at[i],
            device_id=to, device_id_type=MESH,
        )
        copy.start()
        sent.append(copy)
        return copy

    def local(src, dst):
        i = used[1]
        used[1] += 1
        assert i < N_LOCAL
        copy = pltpu.make_async_copy(src, dst, lsem.at[i])
        copy.start()
        return copy

    own_rows = pl.ds(pl.multiple_of(t * TOK, TOK), TOK)

    lx = local(x_hbm.at[0], xs)
    lh = local(h_hbm.at[0], hs)
    lg = local(g_hbm.at[0], gf.at[own_rows])
    lwo = local(wout_hbm.at[0], wout)
    lwi = local(win_hbm.at[0], win)

    barrier = pltpu.get_barrier_semaphore()
    for to in (core_dev, chip_dev, diag_dev, xp, xm, yp, ym, z_down, z_up):
        pl.semaphore_signal(barrier, inc=1, device_id=to, device_id_type=MESH)
    pl.semaphore_wait(barrier, 9)

    def block_cols(k):
        return pl.ds(pl.multiple_of(((xi + k) % 4) * XB, XB), XB)

    order = (2, 1, 3, 0)
    chip_rows = pl.ds(pl.multiple_of(((t + 2) % 4) * TOK, TOK), TOK)

    def pass_on(copies, full, k):
        copies[k].wait_recv()
        chip_block = full.at[chip_rows, block_cols(k)]
        return remote(chip_block, chip_block, core_dev)

    def send_g(k, to):
        return remote(g_hbm.at[0, :, block_cols(k)], gf.at[own_rows, block_cols(k)], to)

    g_chip = {2: send_g(2, chip_dev)}
    slot = plan_ref[0]
    lx.wait()
    halo[0] = xs[slot, TOK - 16 :, :]
    halo[1] = xs[slot, :16, :]
    h_next = remote(halo.at[0], halo.at[2], seq_next)
    h_prev = remote(halo.at[1], halo.at[3], seq_prev)
    for k in order[1:]:
        g_chip[k] = send_g(k, chip_dev)
    g_core = {k: send_g(k, core_dev) for k in order}

    def widen(i, carry):
        rows = pl.ds(pl.multiple_of(i * 16, 16), 16)
        xw[pl.ds(pl.multiple_of(16 + i * 16, 16), 16), :] = xs[slot, rows, :].astype(f32)
        return carry

    lax.fori_loop(0, TOK // 16, widen, 0)

    lh.wait()

    def gelu_rows(i, carry):
        rows = pl.ds(pl.multiple_of(i * 16, 16), 16)
        hv = hs[slot, rows, :].astype(f32)
        square = hv * hv
        tangent = jnp.tanh(root_coef * hv * (1.0 + gelu_coef * square))
        half = 0.5 + 0.5 * tangent
        value = hv * half
        active[rows, :] = value.astype(bf16)
        slope[rows, :] = half + value * (1.0 - tangent) * (
            root_coef + (3.0 * gelu_coef * root_coef) * square
        )
        return carry

    lax.fori_loop(0, SEQ // 16, gelu_rows, 0)

    h_next.wait_recv()
    h_prev.wait_recv()
    xw[0:16, :] = jnp.where(t > 0, halo[2].astype(f32), 0.0)
    xw[16 + TOK : 32 + TOK, :] = jnp.where(t < 3, halo[3].astype(f32), 0.0)

    def norm_rows(first, count):
        near = xw[pl.ds(first, count + 16), :]
        out = cb_ref[...] + cw_ref[0] * near[5 : 5 + count]
        for k in range(1, KER):
            out = out + cw_ref[k] * near[5 + k : 5 + k + count]
        center = out - jnp.mean(out, -1, keepdims=True)
        istd = lax.rsqrt(jnp.mean(center * center, -1, keepdims=True) + norm_eps)
        return center * istd, istd

    def own_norm(i, carry):
        rows = pl.ds(pl.multiple_of(i * 16, 16), 16)
        value, istd = norm_rows(pl.multiple_of(16 * i + 8, 8), 16)
        normed[rows, :] = value
        inv[rows, :] = jnp.broadcast_to(istd, (16, 128))
        sf[pl.ds(pl.multiple_of(t * TOK + i * 16, 16), 16), :] = (
            value * gain_ref[...] + shift_ref[...]
        ).astype(bf16)
        return carry

    lax.fori_loop(0, TOK // 32, own_norm, 0)
    g_pass = {2: pass_on(g_chip, gf, 2)}
    lax.fori_loop(TOK // 32, TOK // 16, own_norm, 0)

    def send_s(k, to):
        own_block = sf.at[own_rows, block_cols(k)]
        return remote(own_block, own_block, to)

    s_chip = {k: send_s(k, chip_dev) for k in order}
    s_core = {k: send_s(k, core_dev) for k in order}
    def hidden_grads(half):
        base = pl.multiple_of(half * 256, 256)
        for j in range(2):
            cols = pl.ds(j * CH, CH)
            d = dot_nt(gf[pl.ds(base, 256), :], wout[j * CH : (j + 1) * CH, :])
            d = d * slope[pl.ds(base, 256), cols]
            bias[:, cols] += jnp.sum(d, 0, keepdims=True)
            dh[pl.ds(base, 256), cols] = d.astype(bf16)

    def part_scaled(half):
        base = pl.multiple_of(half * 256, 256)

        def block(j, carry):
            cols = pl.ds(pl.multiple_of(j * CH, CH), CH)
            dpart[pl.ds(pl.multiple_of(base + 8, 8), 256), cols] = dot_nt(
                dh[pl.ds(base, 256), :], win[cols, :]
            )
            return carry

        lax.fori_loop(0, D // CH, block, 0)

    def weight_part(c, k, src, hidden):
        block = dot_tn(src[:, block_cols(k)], hidden[...]).astype(bf16)
        part[c, k] = block[:, :CH]
        part[c + 1, k] = block[:, CH:]

    def ring_far(own, two, half, plus, minus):
        far_a = remote(own.at[2, pl.ds(0, half)], two.at[0], plus)
        far_b = remote(own.at[2, pl.ds(half, half)], two.at[1], minus)
        return far_a, far_b

    def ring_near(own, last, half, plus, minus):
        near_b = remote(own.at[1, pl.ds(half, half)], last.at[0, pl.ds(half, half)], plus)
        near_a = remote(own.at[3, pl.ds(0, half)], last.at[1, pl.ds(0, half)], minus)
        return near_a, near_b

    def ring_second(copies, own, two, last, half, plus, minus):
        far_a, far_b, near_a, near_b = copies
        far_a.wait_recv()

        def add_a(i, carry):
            rows = pl.ds(pl.multiple_of(i * 48, 16), 48)
            own[1, rows, :] = (own[1, rows, :].astype(f32) + two[0, rows, :].astype(f32)).astype(bf16)
            return carry

        lax.fori_loop(0, half // 48, add_a, 0)
        sum_a = remote(own.at[1, pl.ds(0, half)], last.at[0, pl.ds(0, half)], plus)
        far_b.wait_recv()

        def add_b(i, carry):
            rows = pl.ds(pl.multiple_of(half + i * 48, 16), 48)
            here = pl.ds(pl.multiple_of(i * 48, 16), 48)
            own[3, rows, :] = (own[3, rows, :].astype(f32) + two[1, here, :].astype(f32)).astype(bf16)
            return carry

        lax.fori_loop(0, half // 48, add_b, 0)
        sum_b = remote(own.at[3, pl.ds(half, half)], last.at[1, pl.ds(half, half)], minus)
        return near_a, near_b, sum_a, sum_b

    x_copies, y_copies = {}, {}

    def x_far(c):
        x_copies[c] = ring_far(part.at[c], xr2.at[c], XB // 2, xp, xm)

    def x_near(c):
        x_copies[c] += ring_near(part.at[c], xrx.at[c], XB // 2, xp, xm)

    def x_second(c):
        x_copies[c] = ring_second(x_copies[c], part.at[c], xr2.at[c], xrx.at[c], XB // 2, xp, xm)

    def x_third(c):
        for copy in x_copies[c]:
            copy.wait_recv()

        def block(k, carry):
            for piece in range(2):
                rows = pl.ds(pl.multiple_of(((yi + k) % 4) * YB + piece * 48, 16), 48)
                q[c, k, pl.ds(piece * 48, 48), :] = (
                    part[c, 0, rows, :].astype(f32)
                    + xrx[c, 0, rows, :].astype(f32)
                    + xrx[c, 1, rows, :].astype(f32)
                ).astype(bf16)
            return carry

        lax.fori_loop(0, 4, block, 0)

    def y_first(c):
        y_copies[c] = ring_far(q.at[c], yr2.at[c], YB // 2, yp, ym)
        y_copies[c] += ring_near(q.at[c], yrx.at[c], YB // 2, yp, ym)

    def y_second(c):
        y_copies[c] = ring_second(y_copies[c], q.at[c], yr2.at[c], yrx.at[c], YB // 2, yp, ym)

    def y_third(c):
        for copy in y_copies[c]:
            copy.wait_recv()
        out = gwo_out if c < 2 else gwi_out
        for piece in range(2):
            rows = pl.ds(piece * 48, 48)
            out[rows, pl.ds((c % 2) * CH, CH)] = (
                q[c, 0, rows, :].astype(f32)
                + yrx[c, 0, rows, :].astype(f32)
                + yrx[c, 1, rows, :].astype(f32)
            )

    lg.wait()
    for k in order:
        g_core[k].wait_recv()
    g_pass[2].wait_recv()
    weight_part(0, 2, gf, active)
    x_far(0)
    x_far(1)

    for first, row in ((0, TOK), (TOK + 8, TOK + 8)):
        value, istd = norm_rows(first, 8)
        normed[row : row + 8, :] = value
        inv[row : row + 8, :] = jnp.broadcast_to(istd, (8, 128))

    bias[...] = jnp.zeros_like(bias)
    dpart[0:8, :] = jnp.zeros((8, D), f32)
    dpart[SEQ + 8 : SEQ + 16, :] = jnp.zeros((8, D), f32)
    lwo.wait()
    hidden_grads(ylo)
    g_pass[1] = pass_on(g_chip, gf, 1)
    lwi.wait()
    part_scaled(ylo)

    g_pass[3] = pass_on(g_chip, gf, 3)
    g_pass[1].wait_recv()
    weight_part(0, 1, gf, active)
    g_pass[0] = pass_on(g_chip, gf, 0)
    g_pass[3].wait_recv()
    weight_part(0, 3, gf, active)
    x_near(0)
    x_near(1)
    g_pass[0].wait_recv()
    hidden_grads(1 - ylo)
    part_scaled(1 - ylo)

    def target_rows(tt, i):
        return dpart[pl.ds(pl.multiple_of(8 + tt * TOK + i * 16, 8), 16), :]

    def target_rim(tt, after):
        return dpart[pl.ds(pl.multiple_of(tt * TOK + after * (TOK + 8), 8), 8), :]

    core_far = (1 - ylo) * 2 + 1 - core
    core_near = ylo * 2 + 1 - core
    core_sums = []
    for n, tt in enumerate((core_far, core_near)):

        def fill(i, carry, n=n, tt=tt):
            s1[n, pl.ds(pl.multiple_of(i * 16, 16), 16), :] = target_rows(tt, i).astype(bf16)
            return carry

        lax.fori_loop(0, TOK // 16, fill, 0)
        s1[n, TOK:, :] = jnp.concatenate([target_rim(tt, 0), target_rim(tt, 1)], 0).astype(bf16)
        core_sums.append(remote(s1.at[n], r1.at[n], core_dev))

    weight_part(0, 0, gf, active)
    x_second(0)

    core_sums[0].wait_recv()
    chip_t = (t + 2) % 4

    def add_far(i, carry):
        rows = pl.ds(pl.multiple_of(i * 16, 16), 16)
        s2[rows, :] = (target_rows(chip_t, i) + r1[0, rows, :].astype(f32)).astype(bf16)
        return carry

    lax.fori_loop(0, TOK // 16, add_far, 0)
    s2[TOK:, :] = (
        jnp.concatenate([target_rim(chip_t, 0), target_rim(chip_t, 1)], 0) + r1[0, TOK:, :].astype(f32)
    ).astype(bf16)
    far_sum = remote(s2, r2t, chip_dev)

    x_second(1)
    s_pass = {2: pass_on(s_chip, sf, 2)}
    for k in order:
        s_core[k].wait_recv()
    s_pass[2].wait_recv()
    weight_part(2, 2, sf, dh)
    x_far(2)
    x_far(3)
    for k in order[1:]:
        s_pass[k] = pass_on(s_chip, sf, k)
    s_pass[1].wait_recv()
    weight_part(2, 1, sf, dh)
    s_pass[3].wait_recv()
    weight_part(2, 3, sf, dh)
    x_near(2)
    x_near(3)
    s_pass[0].wait_recv()
    weight_part(2, 0, sf, dh)
    x_third(0)
    y_first(0)
    x_third(1)
    y_first(1)

    core_sums[1].wait_recv()
    far_sum.wait_recv()
    accs[...] = jnp.zeros_like(accs)

    def norm_back(ds, rows, count):
        nv = normed[rows, :]
        dn = ds * gain_ref[...]
        mean_d = jnp.mean(dn, -1, keepdims=True)
        mean_p = jnp.mean(dn * nv, -1, keepdims=True)
        return nv, inv[rows, 0:1] * (dn - mean_d - nv * mean_p)

    def own_back(i, carry):
        rows = pl.ds(pl.multiple_of(i * 16, 16), 16)
        ds = target_rows(t, i) + r1[1, rows, :].astype(f32) + r2t[rows, :].astype(f32)
        nv, dm = norm_back(ds, rows, 16)
        dmix[pl.ds(pl.multiple_of(8 + i * 16, 8), 16), :] = dm
        dsn = ds * nv
        accs[0] += dsn[0:8] + dsn[8:16]
        accs[1] += ds[0:8] + ds[8:16]
        return carry

    lax.fori_loop(0, TOK // 16, own_back, 0)
    rim = pl.ds(TOK, 16)
    rim_ds = (
        jnp.concatenate([target_rim(t, 0), target_rim(t, 1)], 0)
        + r1[1, TOK:, :].astype(f32)
        + r2t[TOK:, :].astype(f32)
    )
    _, rim_dm = norm_back(rim_ds, rim, 16)
    dmix[0:8, :] = rim_dm[0:8]
    dmix[TOK + 8 : TOK + 16, :] = rim_dm[8:16]


    def input_rows(i, carry):
        near = dmix[pl.ds(pl.multiple_of(16 * i, 16), 32), :]
        d = cw_ref[0] * near[11:27]
        for k in range(1, KER):
            d = d + cw_ref[k] * near[11 - k : 27 - k]
        gv = gf[pl.ds(pl.multiple_of(t * TOK + i * 16, 16), 16), :].astype(f32)
        gx[pl.ds(pl.multiple_of(i * 16, 16), 16), :] = jnp.where(pz > 0, gv + d, 0.0).astype(bf16)
        return carry

    z_copies = []
    for piece in range(2):
        lax.fori_loop(piece * 4, piece * 4 + 4, input_rows, 0)
        rows = pl.ds(piece * 64, 64)
        z_copies.append(remote(gx.at[rows], gin_out.at[0, rows], z_down))

    sm[...] = jnp.zeros_like(sm)

    def tap_sums(j, carry):
        cols = pl.ds(pl.multiple_of(j * 256, 256), 256)

        def rows_step(i, totals):
            dm = dmix[pl.ds(pl.multiple_of(8 + 8 * i, 8), 8), cols]
            near = xw[pl.ds(pl.multiple_of(8 + 8 * i, 8), 24), cols]
            out = [totals[k] + dm * near[5 + k : 13 + k] for k in range(KER)]
            out.append(totals[KER] + dm)
            return tuple(out)

        totals = lax.fori_loop(
            0, TOK // 8, rows_step, tuple(jnp.zeros((8, 256), f32) for _ in range(KER + 1))
        )
        for k in range(KER + 1):
            sm[k : k + 1, cols] = jnp.sum(totals[k], 0, keepdims=True)

        def g_step(i, total):
            gv = gf[pl.ds(pl.multiple_of(t * TOK + i * 16, 16), 16), cols].astype(f32)
            return total + gv[0:8] + gv[8:16]

        total = lax.fori_loop(0, TOK // 16, g_step, jnp.zeros((8, 256), f32))
        sm[10:11, cols] = jnp.sum(total, 0, keepdims=True)
        sm[8:9, cols] = jnp.sum(accs[0, :, cols], 0, keepdims=True)
        sm[9:10, cols] = jnp.sum(accs[1, :, cols], 0, keepdims=True)
        return carry

    lax.fori_loop(0, D // 256, tap_sums, 0)
    zero_row = jnp.zeros((1, HID), f32)
    for s in range(4):
        sm[11 + s // 2 : 12 + s // 2, (s % 2) * HID : (s % 2 + 1) * HID] = jnp.where(
            t == s, bias[...], zero_row
        )
    a_core = remote(sm, arc, core_dev)

    y_second(0)
    y_second(1)
    a_core.wait_recv()
    my8 = pl.ds(pl.multiple_of(core * 8, 8), 8)
    ar[0] = sm[my8, :] + arc[my8, :]
    partners = (chip_dev, x_a, x_b, y_a, y_b)
    a_copy = remote(ar.at[0], arr.at[0], partners[0])

    def a_step(n):
        a_copy.wait_recv()
        ar[n] = ar[n - 1] + arr[n - 1]
        if n < len(partners):
            return remote(ar.at[n], arr.at[n], partners[n])
        return None

    x_second(2)
    x_second(3)
    a_copy = a_step(1)
    y_third(0)
    y_third(1)
    a_copy = a_step(2)
    a_copy = a_step(3)
    x_third(2)
    y_first(2)
    a_copy = a_step(4)
    x_third(3)
    y_first(3)
    a_step(5)
    small_out[my8, :] = ar[5]
    a_back = remote(ar.at[5], small_out.at[my8], core_dev)
    y_second(2)
    y_second(3)
    y_third(2)
    y_third(3)
    a_back.wait_recv()
    for copy in z_copies:
        copy.wait_recv()
    for copy in sent:
        copy.wait_send()


def deliver(gin, gwi, gwo, small, gin_out, gwi_out, gwo_out, conv_out, affine_out, bias_out):
    gin_out[...] = gin[...]
    gwi_out[...] = gwi[...]
    gwo_out[...] = gwo[...]
    conv_out[...] = small[0:8, :]
    for i in range(3):
        affine_out[i] = small[8 + i : 9 + i, :]
    for i in range(2):
        bias_out[:, i * D : (i + 1) * D] = small[11 + i : 12 + i, :]


def per_device(x_stash, h_stash, cotangent, plan, conv_w, conv_b, norm_gain, shift_b, w_in, w_out):
    anyspace = pl.BlockSpec(memory_space=pl.ANY)
    vmem = pl.BlockSpec(memory_space=pltpu.VMEM)
    smem = pl.BlockSpec(memory_space=pltpu.SMEM)
    results = pl.pallas_call(
        kernel,
        out_shape=(
            jax.ShapeDtypeStruct((1, TOK, D), bf16),
            jax.ShapeDtypeStruct((YB, HID), f32),
            jax.ShapeDtypeStruct((YB, HID), f32),
            jax.ShapeDtypeStruct((16, D), f32),
        ),
        in_specs=[anyspace, anyspace, anyspace, smem, vmem, vmem, vmem, vmem, anyspace, anyspace],
        out_specs=(anyspace, vmem, vmem, vmem),
        scratch_shapes=[
            pltpu.VMEM((2, TOK, D), bf16),
            pltpu.VMEM((2, SEQ, HID), bf16),
            pltpu.VMEM((SEQ, D), bf16),
            pltpu.VMEM((SEQ, D), bf16),
            pltpu.VMEM((D, HID), bf16),
            pltpu.VMEM((HID, D), bf16),
            pltpu.VMEM((4, 16, D), bf16),
            pltpu.VMEM((TOK + 32, D), f32),
            pltpu.VMEM((WIDE, D), f32),
            pltpu.VMEM((WIDE, 128), f32),
            pltpu.VMEM((SEQ, HID), bf16),
            pltpu.VMEM((SEQ, HID), f32),
            pltpu.VMEM((SEQ, HID), bf16),
            pltpu.VMEM((SEQ + 16, D), f32),
            pltpu.VMEM((2, WIDE, D), bf16),
            pltpu.VMEM((2, WIDE, D), bf16),
            pltpu.VMEM((WIDE, D), bf16),
            pltpu.VMEM((WIDE, D), bf16),
            pltpu.VMEM((4, 4, XB, CH), bf16),
            pltpu.VMEM((4, 2, XB // 2, CH), bf16),
            pltpu.VMEM((4, 2, XB, CH), bf16),
            pltpu.VMEM((4, 4, YB, CH), bf16),
            pltpu.VMEM((4, 2, YB // 2, CH), bf16),
            pltpu.VMEM((4, 2, YB, CH), bf16),
            pltpu.VMEM((WIDE, D), f32),
            pltpu.VMEM((TOK, D), bf16),
            pltpu.VMEM((2, 8, D), f32),
            pltpu.VMEM((16, D), f32),
            pltpu.VMEM((16, D), f32),
            pltpu.VMEM((6, 8, D), f32),
            pltpu.VMEM((5, 8, D), f32),
            pltpu.VMEM((1, HID), f32),
            pltpu.SemaphoreType.DMA((N_COPIES,)),
            pltpu.SemaphoreType.DMA((N_COPIES,)),
            pltpu.SemaphoreType.DMA((N_LOCAL,)),
        ],
        compiler_params=pltpu.CompilerParams(
            collective_id=0, has_side_effects=True, vmem_limit_bytes=56 * 1024 * 1024
        ),
    )(
        x_stash, h_stash, cotangent, plan, jnp.swapaxes(conv_w, 0, 1), conv_b, norm_gain, shift_b, w_in, w_out
    )
    gin, gwi, gwo, conv, affine, bias = pl.pallas_call(
        deliver,
        out_shape=(
            jax.ShapeDtypeStruct((1, TOK, D), bf16),
            jax.ShapeDtypeStruct((YB, HID), f32),
            jax.ShapeDtypeStruct((YB, HID), f32),
            jax.ShapeDtypeStruct((8, D), f32),
            jax.ShapeDtypeStruct((3, 1, D), f32),
            jax.ShapeDtypeStruct((1, 2 * D), f32),
        ),
        in_specs=[vmem] * 4,
        out_specs=(vmem,) * 6,
    )(*results)
    return (
        gin,
        gwi[None],
        gwo.T[None],
        conv[None],
        jnp.swapaxes(affine, 0, 1),
        bias,
    )


def solution(mesh):
    return jax.shard_map(
        per_device,
        mesh=mesh,
        in_specs=(
            P("pipe", None, ("dp", "tensor"), None),
            P("pipe", None, "dp", "tensor"),
            P("pipe", ("dp", "tensor"), None),
            P("pipe"),
            P("pipe", None, None),
            P("pipe", None),
            P("pipe", None),
            P("pipe", None),
            P("pipe", None, "tensor"),
            P("pipe", "tensor", None),
        ),
        out_specs=(
            P("pipe", ("dp", "tensor"), None),
            P("pipe", "dp", "tensor"),
            P("pipe", "tensor", "dp"),
            P("pipe", None, None),
            P("pipe", None, None),
            P("pipe", None),
        ),
        check_vma=False,
    )
```

```python
import math

import jax
import jax.numpy as jnp
from jax import lax
from jax.experimental import pallas as pl
from jax.experimental.pallas import tpu as pltpu
from jax.sharding import PartitionSpec as P

MESH = pl.DeviceIdType.MESH
f32 = jnp.float32
bf16 = jnp.bfloat16

gelu_coef = 0.044715
root_coef = math.sqrt(2.0 / math.pi)
norm_eps = 1e-06

D = 1536
HID = 768
SEQ = 512
TOK = 128
KER = 7
CH = 384
XB = D // 4
YB = XB // 4
WIDE = TOK + 16
N_COPIES = 112
N_LOCAL = 16


def dot_tn(a, b):
    return lax.dot_general(a, b, (((0,), (0,)), ((), ())), preferred_element_type=f32)


def dot_nt(a, b):
    return lax.dot_general(a, b, (((1,), (1,)), ((), ())), preferred_element_type=f32)


def kernel(
    x_hbm, h_hbm, g_hbm, plan_ref, cw_hbm, cb_hbm, gain_hbm, shift_hbm, win_hbm, wout_hbm,
    gin_out, gwi_out, gwo_out, small_out, cw_ref, cb_ref, gain_ref, shift_ref,
    xs, hs, gf, sf, win, wout, halo, xw, normed, inv, active, slope, dh, dpart, s1, r1, s2, r2t,
    part, xr2, xrx, q, yr2, yrx, dmix, gx, accs, sm, arc, ar, arr, arx, ary, arf, bias, ssem, rsem, lsem,
):
    dp = lax.axis_index("dp")
    pz = lax.axis_index("pipe")
    t = lax.axis_index("tensor")
    xi, yi = dp // 4, dp % 4
    ylo, core = t // 2, t % 2
    npipe = lax.axis_size("pipe")

    def dev(dp_=None, pz_=None, t_=None):
        return (
            dp if dp_ is None else dp_,
            pz if pz_ is None else pz_,
            t if t_ is None else t_,
        )

    core_dev = dev(t_=ylo * 2 + 1 - core)
    chip_dev = dev(t_=(t + 2) % 4)
    diag_dev = dev(t_=(1 - ylo) * 2 + 1 - core)
    seq_next, seq_prev = dev(t_=(t + 1) % 4), dev(t_=(t + 3) % 4)
    xp, xm = dev(dp_=((xi + 1) % 4) * 4 + yi), dev(dp_=((xi + 3) % 4) * 4 + yi)
    yp, ym = dev(dp_=xi * 4 + (yi + 1) % 4), dev(dp_=xi * 4 + (yi + 3) % 4)
    x2, y2 = dev(dp_=((xi + 2) % 4) * 4 + yi), dev(dp_=xi * 4 + (yi + 2) % 4)
    z_down = dev(pz_=(pz + npipe - 1) % npipe)
    z_up = dev(pz_=(pz + 1) % npipe)

    used = [0, 0]
    sent = []

    def remote(src, dst, to):
        i = used[0]
        used[0] += 1
        assert i < N_COPIES
        copy = pltpu.make_async_remote_copy(
            src_ref=src, dst_ref=dst, send_sem=ssem.at[i], recv_sem=rsem.at[i],
            device_id=to, device_id_type=MESH,
        )
        copy.start()
        sent.append(copy)
        return copy

    def local(src, dst):
        i = used[1]
        used[1] += 1
        assert i < N_LOCAL
        copy = pltpu.make_async_copy(src, dst, lsem.at[i])
        copy.start()
        return copy

    own_rows = pl.ds(pl.multiple_of(t * TOK, TOK), TOK)

    barrier = pltpu.get_barrier_semaphore()
    for to in (core_dev, chip_dev, diag_dev, xp, xm, x2, yp, ym, y2, z_down, z_up):
        pl.semaphore_signal(barrier, inc=1, device_id=to, device_id_type=MESH)
    lx = local(x_hbm.at[0], xs)
    lh = local(h_hbm.at[0], hs)
    pl.semaphore_wait(barrier, 11)

    def block_cols(k):
        return pl.ds(pl.multiple_of(((xi + k) % 4) * XB, XB), XB)

    order = (2, 1, 3, 0)
    chip_rows = pl.ds(pl.multiple_of(((t + 2) % 4) * TOK, TOK), TOK)

    def pass_on(copies, full, k):
        copies[k].wait_recv()
        chip_block = full.at[chip_rows, block_cols(k)]
        return remote(chip_block, chip_block, core_dev)

    def send_g(k, to):
        return remote(g_hbm.at[0, :, block_cols(k)], gf.at[own_rows, block_cols(k)], to)

    g_chip = {2: send_g(2, chip_dev)}
    slot = plan_ref[0]
    lx.wait()
    halo[0] = xs[slot, TOK - 16 :, :]
    halo[1] = xs[slot, :16, :]
    h_next = remote(halo.at[0], halo.at[2], seq_next)
    h_prev = remote(halo.at[1], halo.at[3], seq_prev)
    for k in order[1:]:
        g_chip[k] = send_g(k, chip_dev)
    g_core = {k: send_g(k, core_dev) for k in order}
    small_loads = [
        local(cw_hbm, cw_ref), local(cb_hbm, cb_ref), local(gain_hbm, gain_ref), local(shift_hbm, shift_ref)
    ]
    lg = local(g_hbm.at[0], gf.at[own_rows])
    lwo = local(wout_hbm.at[0], wout)
    lwi = local(win_hbm.at[0], win)

    def widen(i, carry):
        rows = pl.ds(pl.multiple_of(i * 16, 16), 16)
        xw[pl.ds(pl.multiple_of(16 + i * 16, 16), 16), :] = xs[slot, rows, :].astype(f32)
        return carry

    lax.fori_loop(0, TOK // 16, widen, 0)

    lh.wait()

    def gelu_rows(i, carry):
        rows = pl.ds(pl.multiple_of(i * 16, 16), 16)
        hv = hs[slot, rows, :].astype(f32)
        square = hv * hv
        tangent = jnp.tanh(root_coef * hv * (1.0 + gelu_coef * square))
        half = 0.5 + 0.5 * tangent
        value = hv * half
        active[rows, :] = value.astype(bf16)
        slope[rows, :] = half + value * (1.0 - tangent) * (
            root_coef + (3.0 * gelu_coef * root_coef) * square
        )
        return carry

    lax.fori_loop(0, SEQ // 16, gelu_rows, 0)

    for copy in small_loads:
        copy.wait()
    h_next.wait_recv()
    h_prev.wait_recv()
    xw[0:16, :] = jnp.where(t > 0, halo[2].astype(f32), 0.0)
    xw[16 + TOK : 32 + TOK, :] = jnp.where(t < 3, halo[3].astype(f32), 0.0)

    def norm_rows(first, count):
        near = xw[pl.ds(first, count + 16), :]
        out = cb_ref[...] + cw_ref[0] * near[5 : 5 + count]
        for k in range(1, KER):
            out = out + cw_ref[k] * near[5 + k : 5 + k + count]
        center = out - jnp.mean(out, -1, keepdims=True)
        istd = lax.rsqrt(jnp.mean(center * center, -1, keepdims=True) + norm_eps)
        return center * istd, istd

    def own_norm(i, carry):
        rows = pl.ds(pl.multiple_of(i * 16, 16), 16)
        value, istd = norm_rows(pl.multiple_of(16 * i + 8, 8), 16)
        normed[rows, :] = value
        inv[rows, :] = jnp.broadcast_to(istd, (16, 128))
        sf[pl.ds(pl.multiple_of(t * TOK + i * 16, 16), 16), :] = (
            value * gain_ref[...] + shift_ref[...]
        ).astype(bf16)
        return carry

    lax.fori_loop(0, TOK // 32, own_norm, 0)
    g_pass = {2: pass_on(g_chip, gf, 2)}
    lax.fori_loop(TOK // 32, TOK // 16, own_norm, 0)

    def send_s(k, to):
        own_block = sf.at[own_rows, block_cols(k)]
        return remote(own_block, own_block, to)

    s_chip = {k: send_s(k, chip_dev) for k in order}
    s_core = {k: send_s(k, core_dev) for k in order}
    def hidden_grads(half):
        base = pl.multiple_of(half * 256, 256)
        for j in range(2):
            cols = pl.ds(j * CH, CH)
            d = dot_nt(gf[pl.ds(base, 256), :], wout[j * CH : (j + 1) * CH, :])
            d = d * slope[pl.ds(base, 256), cols]
            bias[:, cols] += jnp.sum(d, 0, keepdims=True)
            dh[pl.ds(base, 256), cols] = d.astype(bf16)

    def part_scaled(half):
        base = pl.multiple_of(half * 256, 256)

        def block(j, carry):
            cols = pl.ds(pl.multiple_of(j * CH, CH), CH)
            dpart[pl.ds(pl.multiple_of(base + 8, 8), 256), cols] = dot_nt(
                dh[pl.ds(base, 256), :], win[cols, :]
            )
            return carry

        lax.fori_loop(0, D // CH, block, 0)

    def weight_part(c, k, src, hidden):
        block = dot_tn(src[:, block_cols(k)], hidden[...]).astype(bf16)
        part[c, k] = block[:, :CH]
        part[c + 1, k] = block[:, CH:]

    def ring_far(own, two, half, plus, minus):
        far_a = remote(own.at[2, pl.ds(0, half)], two.at[0], plus)
        far_b = remote(own.at[2, pl.ds(half, half)], two.at[1], minus)
        return far_a, far_b

    def ring_near(own, last, half, plus, minus):
        near_b = remote(own.at[1, pl.ds(half, half)], last.at[0, pl.ds(half, half)], plus)
        near_a = remote(own.at[3, pl.ds(0, half)], last.at[1, pl.ds(0, half)], minus)
        return near_a, near_b

    def ring_second(copies, own, two, last, half, plus, minus):
        far_a, far_b, near_a, near_b = copies
        far_a.wait_recv()

        def add_a(i, carry):
            rows = pl.ds(pl.multiple_of(i * 48, 16), 48)
            own[1, rows, :] = (own[1, rows, :].astype(f32) + two[0, rows, :].astype(f32)).astype(bf16)
            return carry

        lax.fori_loop(0, half // 48, add_a, 0)
        sum_a = remote(own.at[1, pl.ds(0, half)], last.at[0, pl.ds(0, half)], plus)
        far_b.wait_recv()

        def add_b(i, carry):
            rows = pl.ds(pl.multiple_of(half + i * 48, 16), 48)
            here = pl.ds(pl.multiple_of(i * 48, 16), 48)
            own[3, rows, :] = (own[3, rows, :].astype(f32) + two[1, here, :].astype(f32)).astype(bf16)
            return carry

        lax.fori_loop(0, half // 48, add_b, 0)
        sum_b = remote(own.at[3, pl.ds(half, half)], last.at[1, pl.ds(half, half)], minus)
        return near_a, near_b, sum_a, sum_b

    x_copies, y_copies = {}, {}

    def x_far(c):
        x_copies[c] = ring_far(part.at[c], xr2.at[c], XB // 2, xp, xm)

    def x_near(c):
        x_copies[c] += ring_near(part.at[c], xrx.at[c], XB // 2, xp, xm)

    def x_second(c):
        x_copies[c] = ring_second(x_copies[c], part.at[c], xr2.at[c], xrx.at[c], XB // 2, xp, xm)

    def x_third(c):
        for copy in x_copies[c]:
            copy.wait_recv()

        def block(k, carry):
            for piece in range(2):
                rows = pl.ds(pl.multiple_of(((yi + k) % 4) * YB + piece * 48, 16), 48)
                q[c, k, pl.ds(piece * 48, 48), :] = (
                    part[c, 0, rows, :].astype(f32)
                    + xrx[c, 0, rows, :].astype(f32)
                    + xrx[c, 1, rows, :].astype(f32)
                ).astype(bf16)
            return carry

        lax.fori_loop(0, 4, block, 0)

    def y_first(c):
        y_copies[c] = ring_far(q.at[c], yr2.at[c], YB // 2, yp, ym)
        y_copies[c] += ring_near(q.at[c], yrx.at[c], YB // 2, yp, ym)

    def y_second(c):
        y_copies[c] = ring_second(y_copies[c], q.at[c], yr2.at[c], yrx.at[c], YB // 2, yp, ym)

    def y_third(c):
        for copy in y_copies[c]:
            copy.wait_recv()
        out = gwo_out if c < 2 else gwi_out
        for piece in range(2):
            rows = pl.ds(piece * 48, 48)
            out[rows, pl.ds((c % 2) * CH, CH)] = (
                q[c, 0, rows, :].astype(f32)
                + yrx[c, 0, rows, :].astype(f32)
                + yrx[c, 1, rows, :].astype(f32)
            )

    lg.wait()
    for k in order:
        g_core[k].wait_recv()
    g_pass[2].wait_recv()
    weight_part(0, 2, gf, active)
    x_far(0)
    x_far(1)

    for first, row in ((0, TOK), (TOK + 8, TOK + 8)):
        value, istd = norm_rows(first, 8)
        normed[row : row + 8, :] = value
        inv[row : row + 8, :] = jnp.broadcast_to(istd, (8, 128))

    bias[...] = jnp.zeros_like(bias)
    dpart[0:8, :] = jnp.zeros((8, D), f32)
    dpart[SEQ + 8 : SEQ + 16, :] = jnp.zeros((8, D), f32)
    lwo.wait()
    hidden_grads(ylo)
    g_pass[1] = pass_on(g_chip, gf, 1)
    lwi.wait()
    part_scaled(ylo)

    g_pass[3] = pass_on(g_chip, gf, 3)
    g_pass[1].wait_recv()
    weight_part(0, 1, gf, active)
    g_pass[0] = pass_on(g_chip, gf, 0)
    g_pass[3].wait_recv()
    weight_part(0, 3, gf, active)
    x_near(0)
    g_pass[0].wait_recv()
    hidden_grads(1 - ylo)
    part_scaled(1 - ylo)

    def target_rows(tt, i):
        return dpart[pl.ds(pl.multiple_of(8 + tt * TOK + i * 16, 8), 16), :]

    def target_rim(tt, after):
        return dpart[pl.ds(pl.multiple_of(tt * TOK + after * (TOK + 8), 8), 8), :]

    core_far = (1 - ylo) * 2 + 1 - core
    core_near = ylo * 2 + 1 - core
    core_sums = []
    for n, tt in enumerate((core_far, core_near)):

        def fill(i, carry, n=n, tt=tt):
            s1[n, pl.ds(pl.multiple_of(i * 16, 16), 16), :] = target_rows(tt, i).astype(bf16)
            return carry

        lax.fori_loop(0, TOK // 16, fill, 0)
        s1[n, TOK:, :] = jnp.concatenate([target_rim(tt, 0), target_rim(tt, 1)], 0).astype(bf16)
        core_sums.append(remote(s1.at[n], r1.at[n], core_dev))

    weight_part(0, 0, gf, active)
    x_second(0)
    x_near(1)

    core_sums[0].wait_recv()
    chip_t = (t + 2) % 4

    def add_far(i, carry):
        rows = pl.ds(pl.multiple_of(i * 16, 16), 16)
        s2[rows, :] = (target_rows(chip_t, i) + r1[0, rows, :].astype(f32)).astype(bf16)
        return carry

    lax.fori_loop(0, TOK // 16, add_far, 0)
    s2[TOK:, :] = (
        jnp.concatenate([target_rim(chip_t, 0), target_rim(chip_t, 1)], 0) + r1[0, TOK:, :].astype(f32)
    ).astype(bf16)
    far_sum = remote(s2, r2t, chip_dev)

    x_second(1)
    s_pass = {2: pass_on(s_chip, sf, 2)}
    for k in order:
        s_core[k].wait_recv()
    s_pass[2].wait_recv()
    weight_part(2, 2, sf, dh)
    x_far(2)
    for k in order[1:]:
        s_pass[k] = pass_on(s_chip, sf, k)
    s_pass[1].wait_recv()
    weight_part(2, 1, sf, dh)
    s_pass[3].wait_recv()
    weight_part(2, 3, sf, dh)
    x_near(2)
    x_far(3)
    s_pass[0].wait_recv()
    weight_part(2, 0, sf, dh)
    x_third(0)
    y_first(0)

    core_sums[1].wait_recv()
    far_sum.wait_recv()
    accs[...] = jnp.zeros_like(accs)

    def norm_back(ds, rows, count):
        nv = normed[rows, :]
        dn = ds * gain_ref[...]
        mean_d = jnp.mean(dn, -1, keepdims=True)
        mean_p = jnp.mean(dn * nv, -1, keepdims=True)
        return nv, inv[rows, 0:1] * (dn - mean_d - nv * mean_p)

    def own_back(i, carry):
        rows = pl.ds(pl.multiple_of(i * 16, 16), 16)
        ds = target_rows(t, i) + r1[1, rows, :].astype(f32) + r2t[rows, :].astype(f32)
        nv, dm = norm_back(ds, rows, 16)
        dmix[pl.ds(pl.multiple_of(8 + i * 16, 8), 16), :] = dm
        dsn = ds * nv
        accs[0] += dsn[0:8] + dsn[8:16]
        accs[1] += ds[0:8] + ds[8:16]
        return carry

    lax.fori_loop(0, TOK // 16, own_back, 0)
    rim = pl.ds(TOK, 16)
    rim_ds = (
        jnp.concatenate([target_rim(t, 0), target_rim(t, 1)], 0)
        + r1[1, TOK:, :].astype(f32)
        + r2t[TOK:, :].astype(f32)
    )
    _, rim_dm = norm_back(rim_ds, rim, 16)
    dmix[0:8, :] = rim_dm[0:8]
    dmix[TOK + 8 : TOK + 16, :] = rim_dm[8:16]


    def input_rows(i, carry):
        near = dmix[pl.ds(pl.multiple_of(16 * i, 16), 32), :]
        d = cw_ref[0] * near[11:27]
        for k in range(1, KER):
            d = d + cw_ref[k] * near[11 - k : 27 - k]
        gv = gf[pl.ds(pl.multiple_of(t * TOK + i * 16, 16), 16), :].astype(f32)
        gx[pl.ds(pl.multiple_of(i * 16, 16), 16), :] = jnp.where(pz > 0, gv + d, 0.0).astype(bf16)
        return carry

    z_copies = []
    for piece in range(2):
        lax.fori_loop(piece * 4, piece * 4 + 4, input_rows, 0)
        rows = pl.ds(piece * 64, 64)
        z_copies.append(remote(gx.at[rows], gin_out.at[0, rows], z_down))

    sm[...] = jnp.zeros_like(sm)

    def tap_sums(j, carry):
        cols = pl.ds(pl.multiple_of(j * 256, 256), 256)

        def rows_step(i, totals):
            dm = dmix[pl.ds(pl.multiple_of(8 + 8 * i, 8), 8), cols]
            near = xw[pl.ds(pl.multiple_of(8 + 8 * i, 8), 24), cols]
            out = [totals[k] + dm * near[5 + k : 13 + k] for k in range(KER)]
            out.append(totals[KER] + dm)
            return tuple(out)

        totals = lax.fori_loop(
            0, TOK // 8, rows_step, tuple(jnp.zeros((8, 256), f32) for _ in range(KER + 1))
        )
        for k in range(KER + 1):
            sm[k : k + 1, cols] = jnp.sum(totals[k], 0, keepdims=True)

        def g_step(i, total):
            gv = gf[pl.ds(pl.multiple_of(t * TOK + i * 16, 16), 16), cols].astype(f32)
            return total + gv[0:8] + gv[8:16]

        total = lax.fori_loop(0, TOK // 16, g_step, jnp.zeros((8, 256), f32))
        sm[10:11, cols] = jnp.sum(total, 0, keepdims=True)
        sm[8:9, cols] = jnp.sum(accs[0, :, cols], 0, keepdims=True)
        sm[9:10, cols] = jnp.sum(accs[1, :, cols], 0, keepdims=True)
        return carry

    lax.fori_loop(0, D // 256, tap_sums, 0)
    zero_row = jnp.zeros((1, HID), f32)
    for s in range(4):
        sm[11 + s // 2 : 12 + s // 2, (s % 2) * HID : (s % 2 + 1) * HID] = jnp.where(
            t == s, bias[...], zero_row
        )
    a_core = remote(sm, arc, core_dev)

    x_second(2)
    x_near(3)
    a_core.wait_recv()
    my8 = pl.ds(pl.multiple_of(core * 8, 8), 8)
    ar[...] = sm[my8, :] + arc[my8, :]
    a_chip = remote(ar, arr, chip_dev)
    x_third(1)
    y_first(1)
    y_second(0)
    x_second(3)
    a_chip.wait_recv()
    arx[xi] = ar[...] + arr[...]
    a_x = [remote(arx.at[xi], arx.at[xi], to) for to in (xp, xm, x2)]
    y_third(0)
    y_second(1)
    x_third(2)
    y_first(2)
    y_third(1)
    for copy in a_x:
        copy.wait_recv()
    ary[yi] = (arx[0] + arx[1]) + (arx[2] + arx[3])
    a_y = [remote(ary.at[yi], ary.at[yi], to) for to in (yp, ym, y2)]
    x_third(3)
    y_first(3)
    y_second(2)
    for copy in a_y:
        copy.wait_recv()
    arf[...] = (ary[0] + ary[1]) + (ary[2] + ary[3])
    small_out[my8, :] = arf[...]
    a_back = remote(arf, small_out.at[my8], core_dev)
    y_second(3)
    y_third(2)
    y_third(3)
    a_back.wait_recv()
    for copy in z_copies:
        copy.wait_recv()
    for copy in sent:
        copy.wait_send()


def deliver(gin, gwi, gwo, small, gin_out, gwi_out, gwo_out, conv_out, affine_out, bias_out):
    gin_out[...] = gin[...]
    gwi_out[...] = gwi[...]
    gwo_out[...] = gwo[...]
    conv_out[...] = small[0:8, :]
    for i in range(3):
        affine_out[i] = small[8 + i : 9 + i, :]
    for i in range(2):
        bias_out[:, i * D : (i + 1) * D] = small[11 + i : 12 + i, :]


def per_device(x_stash, h_stash, cotangent, plan, conv_w, conv_b, norm_gain, shift_b, w_in, w_out):
    anyspace = pl.BlockSpec(memory_space=pl.ANY)
    vmem = pl.BlockSpec(memory_space=pltpu.VMEM)
    smem = pl.BlockSpec(memory_space=pltpu.SMEM)
    results = pl.pallas_call(
        kernel,
        out_shape=(
            jax.ShapeDtypeStruct((1, TOK, D), bf16),
            jax.ShapeDtypeStruct((YB, HID), f32),
            jax.ShapeDtypeStruct((YB, HID), f32),
            jax.ShapeDtypeStruct((16, D), f32),
        ),
        in_specs=[anyspace, anyspace, anyspace, smem] + [anyspace] * 6,
        out_specs=(anyspace, vmem, vmem, vmem),
        scratch_shapes=[
            pltpu.VMEM((KER, 1, D), f32),
            pltpu.VMEM((1, D), f32),
            pltpu.VMEM((1, D), f32),
            pltpu.VMEM((1, D), f32),
            pltpu.VMEM((2, TOK, D), bf16),
            pltpu.VMEM((2, SEQ, HID), bf16),
            pltpu.VMEM((SEQ, D), bf16),
            pltpu.VMEM((SEQ, D), bf16),
            pltpu.VMEM((D, HID), bf16),
            pltpu.VMEM((HID, D), bf16),
            pltpu.VMEM((4, 16, D), bf16),
            pltpu.VMEM((TOK + 32, D), f32),
            pltpu.VMEM((WIDE, D), f32),
            pltpu.VMEM((WIDE, 128), f32),
            pltpu.VMEM((SEQ, HID), bf16),
            pltpu.VMEM((SEQ, HID), f32),
            pltpu.VMEM((SEQ, HID), bf16),
            pltpu.VMEM((SEQ + 16, D), f32),
            pltpu.VMEM((2, WIDE, D), bf16),
            pltpu.VMEM((2, WIDE, D), bf16),
            pltpu.VMEM((WIDE, D), bf16),
            pltpu.VMEM((WIDE, D), bf16),
            pltpu.VMEM((4, 4, XB, CH), bf16),
            pltpu.VMEM((4, 2, XB // 2, CH), bf16),
            pltpu.VMEM((4, 2, XB, CH), bf16),
            pltpu.VMEM((4, 4, YB, CH), bf16),
            pltpu.VMEM((4, 2, YB // 2, CH), bf16),
            pltpu.VMEM((4, 2, YB, CH), bf16),
            pltpu.VMEM((WIDE, D), f32),
            pltpu.VMEM((TOK, D), bf16),
            pltpu.VMEM((2, 8, D), f32),
            pltpu.VMEM((16, D), f32),
            pltpu.VMEM((16, D), f32),
            pltpu.VMEM((8, D), f32),
            pltpu.VMEM((8, D), f32),
            pltpu.VMEM((4, 8, D), f32),
            pltpu.VMEM((4, 8, D), f32),
            pltpu.VMEM((8, D), f32),
            pltpu.VMEM((1, HID), f32),
            pltpu.SemaphoreType.DMA((N_COPIES,)),
            pltpu.SemaphoreType.DMA((N_COPIES,)),
            pltpu.SemaphoreType.DMA((N_LOCAL,)),
        ],
        compiler_params=pltpu.CompilerParams(
            collective_id=0, has_side_effects=True, vmem_limit_bytes=56 * 1024 * 1024
        ),
    )(
        x_stash, h_stash, cotangent, plan, jnp.swapaxes(conv_w, 0, 1), conv_b, norm_gain, shift_b, w_in, w_out
    )
    gin, gwi, gwo, conv, affine, bias = pl.pallas_call(
        deliver,
        out_shape=(
            jax.ShapeDtypeStruct((1, TOK, D), bf16),
            jax.ShapeDtypeStruct((YB, HID), f32),
            jax.ShapeDtypeStruct((YB, HID), f32),
            jax.ShapeDtypeStruct((8, D), f32),
            jax.ShapeDtypeStruct((3, 1, D), f32),
            jax.ShapeDtypeStruct((1, 2 * D), f32),
        ),
        in_specs=[vmem] * 4,
        out_specs=(vmem,) * 6,
    )(*results)
    return (
        gin,
        gwi[None],
        gwo.T[None],
        conv[None],
        jnp.swapaxes(affine, 0, 1),
        bias,
    )


def solution(mesh):
    return jax.shard_map(
        per_device,
        mesh=mesh,
        in_specs=(
            P("pipe", None, ("dp", "tensor"), None),
            P("pipe", None, "dp", "tensor"),
            P("pipe", ("dp", "tensor"), None),
            P("pipe"),
            P("pipe", None, None),
            P("pipe", None),
            P("pipe", None),
            P("pipe", None),
            P("pipe", None, "tensor"),
            P("pipe", "tensor", None),
        ),
        out_specs=(
            P("pipe", ("dp", "tensor"), None),
            P("pipe", "dp", "tensor"),
            P("pipe", "tensor", "dp"),
            P("pipe", None, None),
            P("pipe", None, None),
            P("pipe", None),
        ),
        check_vma=False,
    )
```

```python
import math

import jax
import jax.numpy as jnp
from jax import lax
from jax.experimental import pallas as pl
from jax.experimental.pallas import tpu as pltpu
from jax.sharding import PartitionSpec as P

MESH = pl.DeviceIdType.MESH
f32 = jnp.float32
bf16 = jnp.bfloat16

gelu_coef = 0.044715
root_coef = math.sqrt(2.0 / math.pi)
norm_eps = 1e-06

D = 1536
HID = 768
SEQ = 512
TOK = 128
KER = 7
CH = 384
XB = D // 4
YB = XB // 4
WIDE = TOK + 16
N_COPIES = 112
CHUNKS = ((0, 256), (256, 512), (0, 512), (512, 256))
N_LOCAL = 16


def dot_tn(a, b):
    return lax.dot_general(a, b, (((0,), (0,)), ((), ())), preferred_element_type=f32)


def dot_nt(a, b):
    return lax.dot_general(a, b, (((1,), (1,)), ((), ())), preferred_element_type=f32)


def kernel(
    x_hbm, h_hbm, g_hbm, plan_ref, cw_hbm, cb_hbm, gain_hbm, shift_hbm, win_hbm, wout_hbm,
    gin_out, gwi_out, gwo_out, small_out, cw_ref, cb_ref, gain_ref, shift_ref,
    xs, hs, gf, sf, win, wout, halo, xw, normed, inv, active, slope, dh, dpart, s1, r1, s2, r2t,
    part, xr2, xrx, q, yr2, yrx, dmix, gx, accs, sm, arc, ar, arr, arx, ary, arf, bias, ssem, rsem, lsem,
):
    dp = lax.axis_index("dp")
    pz = lax.axis_index("pipe")
    t = lax.axis_index("tensor")
    xi, yi = dp // 4, dp % 4
    ylo, core = t // 2, t % 2
    npipe = lax.axis_size("pipe")

    def dev(dp_=None, pz_=None, t_=None):
        return (
            dp if dp_ is None else dp_,
            pz if pz_ is None else pz_,
            t if t_ is None else t_,
        )

    core_dev = dev(t_=ylo * 2 + 1 - core)
    chip_dev = dev(t_=(t + 2) % 4)
    diag_dev = dev(t_=(1 - ylo) * 2 + 1 - core)
    seq_next, seq_prev = dev(t_=(t + 1) % 4), dev(t_=(t + 3) % 4)
    xp, xm = dev(dp_=((xi + 1) % 4) * 4 + yi), dev(dp_=((xi + 3) % 4) * 4 + yi)
    yp, ym = dev(dp_=xi * 4 + (yi + 1) % 4), dev(dp_=xi * 4 + (yi + 3) % 4)
    x2, y2 = dev(dp_=((xi + 2) % 4) * 4 + yi), dev(dp_=xi * 4 + (yi + 2) % 4)
    z_down = dev(pz_=(pz + npipe - 1) % npipe)
    z_up = dev(pz_=(pz + 1) % npipe)

    used = [0, 0]
    sent = []

    def remote(src, dst, to):
        i = used[0]
        used[0] += 1
        assert i < N_COPIES
        copy = pltpu.make_async_remote_copy(
            src_ref=src, dst_ref=dst, send_sem=ssem.at[i], recv_sem=rsem.at[i],
            device_id=to, device_id_type=MESH,
        )
        copy.start()
        sent.append(copy)
        return copy

    def local(src, dst):
        i = used[1]
        used[1] += 1
        assert i < N_LOCAL
        copy = pltpu.make_async_copy(src, dst, lsem.at[i])
        copy.start()
        return copy

    own_rows = pl.ds(pl.multiple_of(t * TOK, TOK), TOK)

    barrier = pltpu.get_barrier_semaphore()
    for to in (core_dev, chip_dev, diag_dev, xp, xm, x2, yp, ym, y2, z_down, z_up):
        pl.semaphore_signal(barrier, inc=1, device_id=to, device_id_type=MESH)
    lx = local(x_hbm.at[0], xs)
    lh = local(h_hbm.at[0], hs)
    pl.semaphore_wait(barrier, 11)

    def block_cols(k):
        return pl.ds(pl.multiple_of(((xi + k) % 4) * XB, XB), XB)

    order = (2, 1, 3, 0)
    chip_rows = pl.ds(pl.multiple_of(((t + 2) % 4) * TOK, TOK), TOK)

    def pass_on(copies, full, k):
        copies[k].wait_recv()
        chip_block = full.at[chip_rows, block_cols(k)]
        return remote(chip_block, chip_block, core_dev)

    def send_g(k, to):
        return remote(g_hbm.at[0, :, block_cols(k)], gf.at[own_rows, block_cols(k)], to)

    g_chip = {2: send_g(2, chip_dev)}
    slot = plan_ref[0]
    lx.wait()
    halo[0] = xs[slot, TOK - 16 :, :]
    halo[1] = xs[slot, :16, :]
    h_next = remote(halo.at[0], halo.at[2], seq_next)
    h_prev = remote(halo.at[1], halo.at[3], seq_prev)
    for k in order[1:]:
        g_chip[k] = send_g(k, chip_dev)
    g_core = {k: send_g(k, core_dev) for k in order}
    small_loads = [
        local(cw_hbm, cw_ref), local(cb_hbm, cb_ref), local(gain_hbm, gain_ref), local(shift_hbm, shift_ref)
    ]
    lg = local(g_hbm.at[0], gf.at[own_rows])
    lwo = local(wout_hbm.at[0], wout)
    lwi = local(win_hbm.at[0], win)

    def widen(i, carry):
        rows = pl.ds(pl.multiple_of(i * 16, 16), 16)
        xw[pl.ds(pl.multiple_of(16 + i * 16, 16), 16), :] = xs[slot, rows, :].astype(f32)
        return carry

    lax.fori_loop(0, TOK // 16, widen, 0)

    lh.wait()

    def gelu_rows(i, carry):
        rows = pl.ds(pl.multiple_of(i * 16, 16), 16)
        hv = hs[slot, rows, :].astype(f32)
        square = hv * hv
        tangent = jnp.tanh(root_coef * hv * (1.0 + gelu_coef * square))
        half = 0.5 + 0.5 * tangent
        value = hv * half
        active[rows, :] = value.astype(bf16)
        slope[rows, :] = half + value * (1.0 - tangent) * (
            root_coef + (3.0 * gelu_coef * root_coef) * square
        )
        return carry

    lax.fori_loop(0, SEQ // 16, gelu_rows, 0)

    for copy in small_loads:
        copy.wait()
    h_next.wait_recv()
    h_prev.wait_recv()
    xw[0:16, :] = jnp.where(t > 0, halo[2].astype(f32), 0.0)
    xw[16 + TOK : 32 + TOK, :] = jnp.where(t < 3, halo[3].astype(f32), 0.0)

    def norm_rows(first, count):
        near = xw[pl.ds(first, count + 16), :]
        out = cb_ref[...] + cw_ref[0] * near[5 : 5 + count]
        for k in range(1, KER):
            out = out + cw_ref[k] * near[5 + k : 5 + k + count]
        center = out - jnp.mean(out, -1, keepdims=True)
        istd = lax.rsqrt(jnp.mean(center * center, -1, keepdims=True) + norm_eps)
        return center * istd, istd

    def own_norm(i, carry):
        rows = pl.ds(pl.multiple_of(i * 16, 16), 16)
        value, istd = norm_rows(pl.multiple_of(16 * i + 8, 8), 16)
        normed[rows, :] = value
        inv[rows, :] = jnp.broadcast_to(istd, (16, 128))
        sf[pl.ds(pl.multiple_of(t * TOK + i * 16, 16), 16), :] = (
            value * gain_ref[...] + shift_ref[...]
        ).astype(bf16)
        return carry

    lax.fori_loop(0, TOK // 32, own_norm, 0)
    g_pass = {2: pass_on(g_chip, gf, 2)}
    lax.fori_loop(TOK // 32, TOK // 16, own_norm, 0)

    def send_s(k, to):
        own_block = sf.at[own_rows, block_cols(k)]
        return remote(own_block, own_block, to)

    s_chip = {k: send_s(k, chip_dev) for k in order}
    s_core = {k: send_s(k, core_dev) for k in order}
    def hidden_grads(half):
        base = pl.multiple_of(half * 256, 256)
        for j in range(2):
            cols = pl.ds(j * CH, CH)
            d = dot_nt(gf[pl.ds(base, 256), :], wout[j * CH : (j + 1) * CH, :])
            d = d * slope[pl.ds(base, 256), cols]
            bias[:, cols] += jnp.sum(d, 0, keepdims=True)
            dh[pl.ds(base, 256), cols] = d.astype(bf16)

    def part_scaled(half):
        base = pl.multiple_of(half * 256, 256)

        def block(j, carry):
            cols = pl.ds(pl.multiple_of(j * CH, CH), CH)
            dpart[pl.ds(pl.multiple_of(base + 8, 8), 256), cols] = dot_nt(
                dh[pl.ds(base, 256), :], win[cols, :]
            )
            return carry

        lax.fori_loop(0, D // CH, block, 0)

    def weight_part(m, k, src, hidden):
        part[m, k] = dot_tn(src[:, block_cols(k)], hidden[...]).astype(bf16)

    def ring_far(own, two, half, cols, plus, minus):
        far_a = remote(own.at[2, pl.ds(0, half), cols], two.at[0, :, cols], plus)
        far_b = remote(own.at[2, pl.ds(half, half), cols], two.at[1, :, cols], minus)
        return far_a, far_b

    def ring_near(own, last, half, cols, plus, minus):
        low, high = pl.ds(0, half), pl.ds(half, half)
        near_b = remote(own.at[1, high, cols], last.at[0, high, cols], plus)
        near_a = remote(own.at[3, low, cols], last.at[1, low, cols], minus)
        return near_a, near_b

    def ring_second(copies, own, two, last, half, cols, plus, minus):
        far_a, far_b, near_a, near_b = copies
        low, high = pl.ds(0, half), pl.ds(half, half)
        far_a.wait_recv()

        def add_a(i, carry):
            rows = pl.ds(pl.multiple_of(i * 48, 16), 48)
            own[1, rows, cols] = (
                own[1, rows, cols].astype(f32) + two[0, rows, cols].astype(f32)
            ).astype(bf16)
            return carry

        lax.fori_loop(0, half // 48, add_a, 0)
        sum_a = remote(own.at[1, low, cols], last.at[0, low, cols], plus)
        far_b.wait_recv()

        def add_b(i, carry):
            rows = pl.ds(pl.multiple_of(half + i * 48, 16), 48)
            here = pl.ds(pl.multiple_of(i * 48, 16), 48)
            own[3, rows, cols] = (
                own[3, rows, cols].astype(f32) + two[1, here, cols].astype(f32)
            ).astype(bf16)
            return carry

        lax.fori_loop(0, half // 48, add_b, 0)
        sum_b = remote(own.at[3, high, cols], last.at[1, high, cols], minus)
        return near_a, near_b, sum_a, sum_b

    x_copies, y_copies = {}, {}

    def chunk(c):
        return c // 2, pl.ds(*CHUNKS[c])

    def x_far(c):
        m, cols = chunk(c)
        x_copies[c] = ring_far(part.at[m], xr2.at[m], XB // 2, cols, xp, xm)

    def x_near(c):
        m, cols = chunk(c)
        x_copies[c] += ring_near(part.at[m], xrx.at[m], XB // 2, cols, xp, xm)

    def x_second(c):
        m, cols = chunk(c)
        x_copies[c] = ring_second(
            x_copies[c], part.at[m], xr2.at[m], xrx.at[m], XB // 2, cols, xp, xm
        )

    def x_third(c):
        m, cols = chunk(c)
        for copy in x_copies[c]:
            copy.wait_recv()

        def block(k, carry):
            for piece in range(2):
                rows = pl.ds(pl.multiple_of(((yi + k) % 4) * YB + piece * 48, 16), 48)
                q[m, k, pl.ds(piece * 48, 48), cols] = (
                    part[m, 0, rows, cols].astype(f32)
                    + xrx[m, 0, rows, cols].astype(f32)
                    + xrx[m, 1, rows, cols].astype(f32)
                ).astype(bf16)
            return carry

        lax.fori_loop(0, 4, block, 0)

    def y_first(c):
        m, cols = chunk(c)
        y_copies[c] = ring_far(q.at[m], yr2.at[m], YB // 2, cols, yp, ym)
        y_copies[c] += ring_near(q.at[m], yrx.at[m], YB // 2, cols, yp, ym)

    def y_second(c):
        m, cols = chunk(c)
        y_copies[c] = ring_second(
            y_copies[c], q.at[m], yr2.at[m], yrx.at[m], YB // 2, cols, yp, ym
        )

    def y_third(c):
        m, cols = chunk(c)
        for copy in y_copies[c]:
            copy.wait_recv()
        out = (gwo_out, gwi_out)[m]
        for piece in range(2):
            rows = pl.ds(piece * 48, 48)
            out[rows, cols] = (
                q[m, 0, rows, cols].astype(f32)
                + yrx[m, 0, rows, cols].astype(f32)
                + yrx[m, 1, rows, cols].astype(f32)
            )

    lg.wait()
    for k in order:
        g_core[k].wait_recv()
    g_pass[2].wait_recv()
    weight_part(0, 2, gf, active)
    x_far(0)
    x_far(1)

    for first, row in ((0, TOK), (TOK + 8, TOK + 8)):
        value, istd = norm_rows(first, 8)
        normed[row : row + 8, :] = value
        inv[row : row + 8, :] = jnp.broadcast_to(istd, (8, 128))

    bias[...] = jnp.zeros_like(bias)
    dpart[0:8, :] = jnp.zeros((8, D), f32)
    dpart[SEQ + 8 : SEQ + 16, :] = jnp.zeros((8, D), f32)
    lwo.wait()
    hidden_grads(ylo)
    g_pass[1] = pass_on(g_chip, gf, 1)
    lwi.wait()
    part_scaled(ylo)

    g_pass[3] = pass_on(g_chip, gf, 3)
    g_pass[1].wait_recv()
    weight_part(0, 1, gf, active)
    g_pass[0] = pass_on(g_chip, gf, 0)
    g_pass[3].wait_recv()
    weight_part(0, 3, gf, active)
    x_near(0)
    g_pass[0].wait_recv()
    hidden_grads(1 - ylo)
    part_scaled(1 - ylo)

    def target_rows(tt, i):
        return dpart[pl.ds(pl.multiple_of(8 + tt * TOK + i * 16, 8), 16), :]

    def target_rim(tt, after):
        return dpart[pl.ds(pl.multiple_of(tt * TOK + after * (TOK + 8), 8), 8), :]

    core_far = (1 - ylo) * 2 + 1 - core
    core_near = ylo * 2 + 1 - core
    core_sums = []
    for n, tt in enumerate((core_far, core_near)):

        def fill(i, carry, n=n, tt=tt):
            s1[n, pl.ds(pl.multiple_of(i * 16, 16), 16), :] = target_rows(tt, i).astype(bf16)
            return carry

        lax.fori_loop(0, TOK // 16, fill, 0)
        s1[n, TOK:, :] = jnp.concatenate([target_rim(tt, 0), target_rim(tt, 1)], 0).astype(bf16)
        core_sums.append(remote(s1.at[n], r1.at[n], core_dev))

    weight_part(0, 0, gf, active)
    x_second(0)
    x_near(1)

    core_sums[0].wait_recv()
    chip_t = (t + 2) % 4

    def add_far(i, carry):
        rows = pl.ds(pl.multiple_of(i * 16, 16), 16)
        s2[rows, :] = (target_rows(chip_t, i) + r1[0, rows, :].astype(f32)).astype(bf16)
        return carry

    lax.fori_loop(0, TOK // 16, add_far, 0)
    s2[TOK:, :] = (
        jnp.concatenate([target_rim(chip_t, 0), target_rim(chip_t, 1)], 0) + r1[0, TOK:, :].astype(f32)
    ).astype(bf16)
    far_sum = remote(s2, r2t, chip_dev)

    x_second(1)
    s_pass = {2: pass_on(s_chip, sf, 2)}
    for k in order:
        s_core[k].wait_recv()
    s_pass[2].wait_recv()
    weight_part(1, 2, sf, dh)
    x_far(2)
    for k in order[1:]:
        s_pass[k] = pass_on(s_chip, sf, k)
    s_pass[1].wait_recv()
    weight_part(1, 1, sf, dh)
    s_pass[3].wait_recv()
    weight_part(1, 3, sf, dh)
    x_near(2)
    x_far(3)
    s_pass[0].wait_recv()
    weight_part(1, 0, sf, dh)
    x_third(0)
    y_first(0)

    core_sums[1].wait_recv()
    far_sum.wait_recv()
    accs[...] = jnp.zeros_like(accs)

    def norm_back(ds, rows, count):
        nv = normed[rows, :]
        dn = ds * gain_ref[...]
        mean_d = jnp.mean(dn, -1, keepdims=True)
        mean_p = jnp.mean(dn * nv, -1, keepdims=True)
        return nv, inv[rows, 0:1] * (dn - mean_d - nv * mean_p)

    def own_back(i, carry):
        rows = pl.ds(pl.multiple_of(i * 16, 16), 16)
        ds = target_rows(t, i) + r1[1, rows, :].astype(f32) + r2t[rows, :].astype(f32)
        nv, dm = norm_back(ds, rows, 16)
        dmix[pl.ds(pl.multiple_of(8 + i * 16, 8), 16), :] = dm
        dsn = ds * nv
        accs[0] += dsn[0:8] + dsn[8:16]
        accs[1] += ds[0:8] + ds[8:16]
        return carry

    lax.fori_loop(0, TOK // 16, own_back, 0)
    rim = pl.ds(TOK, 16)
    rim_ds = (
        jnp.concatenate([target_rim(t, 0), target_rim(t, 1)], 0)
        + r1[1, TOK:, :].astype(f32)
        + r2t[TOK:, :].astype(f32)
    )
    _, rim_dm = norm_back(rim_ds, rim, 16)
    dmix[0:8, :] = rim_dm[0:8]
    dmix[TOK + 8 : TOK + 16, :] = rim_dm[8:16]


    def input_rows(i, carry):
        near = dmix[pl.ds(pl.multiple_of(16 * i, 16), 32), :]
        d = cw_ref[0] * near[11:27]
        for k in range(1, KER):
            d = d + cw_ref[k] * near[11 - k : 27 - k]
        gv = gf[pl.ds(pl.multiple_of(t * TOK + i * 16, 16), 16), :].astype(f32)
        gx[pl.ds(pl.multiple_of(i * 16, 16), 16), :] = jnp.where(pz > 0, gv + d, 0.0).astype(bf16)
        return carry

    z_copies = []
    for piece in range(2):
        lax.fori_loop(piece * 4, piece * 4 + 4, input_rows, 0)
        rows = pl.ds(piece * 64, 64)
        z_copies.append(remote(gx.at[rows], gin_out.at[0, rows], z_down))

    sm[...] = jnp.zeros_like(sm)

    def tap_sums(j, carry):
        cols = pl.ds(pl.multiple_of(j * 256, 256), 256)

        def rows_step(i, totals):
            dm = dmix[pl.ds(pl.multiple_of(8 + 8 * i, 8), 8), cols]
            near = xw[pl.ds(pl.multiple_of(8 + 8 * i, 8), 24), cols]
            out = [totals[k] + dm * near[5 + k : 13 + k] for k in range(KER)]
            out.append(totals[KER] + dm)
            return tuple(out)

        totals = lax.fori_loop(
            0, TOK // 8, rows_step, tuple(jnp.zeros((8, 256), f32) for _ in range(KER + 1))
        )
        for k in range(KER + 1):
            sm[k : k + 1, cols] = jnp.sum(totals[k], 0, keepdims=True)

        def g_step(i, total):
            gv = gf[pl.ds(pl.multiple_of(t * TOK + i * 16, 16), 16), cols].astype(f32)
            return total + gv[0:8] + gv[8:16]

        total = lax.fori_loop(0, TOK // 16, g_step, jnp.zeros((8, 256), f32))
        sm[10:11, cols] = jnp.sum(total, 0, keepdims=True)
        sm[8:9, cols] = jnp.sum(accs[0, :, cols], 0, keepdims=True)
        sm[9:10, cols] = jnp.sum(accs[1, :, cols], 0, keepdims=True)
        return carry

    lax.fori_loop(0, D // 256, tap_sums, 0)
    zero_row = jnp.zeros((1, HID), f32)
    for s in range(4):
        sm[11 + s // 2 : 12 + s // 2, (s % 2) * HID : (s % 2 + 1) * HID] = jnp.where(
            t == s, bias[...], zero_row
        )
    a_core = remote(sm, arc, core_dev)

    x_second(2)
    x_near(3)
    a_core.wait_recv()
    my8 = pl.ds(pl.multiple_of(core * 8, 8), 8)
    ar[...] = sm[my8, :] + arc[my8, :]
    a_chip = remote(ar, arr, chip_dev)
    x_third(1)
    y_first(1)
    y_second(0)
    x_second(3)
    a_chip.wait_recv()
    arx[xi] = ar[...] + arr[...]
    a_x = [remote(arx.at[xi], arx.at[xi], to) for to in (xp, xm, x2)]
    y_third(0)
    y_second(1)
    x_third(2)
    y_first(2)
    y_third(1)
    for copy in a_x:
        copy.wait_recv()
    ary[yi] = (arx[0] + arx[1]) + (arx[2] + arx[3])
    a_y = [remote(ary.at[yi], ary.at[yi], to) for to in (yp, ym, y2)]
    x_third(3)
    y_first(3)
    y_second(2)
    for copy in a_y:
        copy.wait_recv()
    arf[...] = (ary[0] + ary[1]) + (ary[2] + ary[3])
    small_out[my8, :] = arf[...]
    a_back = remote(arf, small_out.at[my8], core_dev)
    y_second(3)
    y_third(2)
    y_third(3)
    a_back.wait_recv()
    for copy in z_copies:
        copy.wait_recv()
    for copy in sent:
        copy.wait_send()


def deliver(gin, gwi, gwo, small, gin_out, gwi_out, gwo_out, conv_out, affine_out, bias_out):
    gin_out[...] = gin[...]
    gwi_out[...] = gwi[...]
    gwo_out[...] = gwo[...]
    conv_out[...] = small[0:8, :]
    for i in range(3):
        affine_out[i] = small[8 + i : 9 + i, :]
    for i in range(2):
        bias_out[:, i * D : (i + 1) * D] = small[11 + i : 12 + i, :]


def per_device(x_stash, h_stash, cotangent, plan, conv_w, conv_b, norm_gain, shift_b, w_in, w_out):
    anyspace = pl.BlockSpec(memory_space=pl.ANY)
    vmem = pl.BlockSpec(memory_space=pltpu.VMEM)
    smem = pl.BlockSpec(memory_space=pltpu.SMEM)
    results = pl.pallas_call(
        kernel,
        out_shape=(
            jax.ShapeDtypeStruct((1, TOK, D), bf16),
            jax.ShapeDtypeStruct((YB, HID), f32),
            jax.ShapeDtypeStruct((YB, HID), f32),
            jax.ShapeDtypeStruct((16, D), f32),
        ),
        in_specs=[anyspace, anyspace, anyspace, smem] + [anyspace] * 6,
        out_specs=(anyspace, vmem, vmem, vmem),
        scratch_shapes=[
            pltpu.VMEM((KER, 1, D), f32),
            pltpu.VMEM((1, D), f32),
            pltpu.VMEM((1, D), f32),
            pltpu.VMEM((1, D), f32),
            pltpu.VMEM((2, TOK, D), bf16),
            pltpu.VMEM((2, SEQ, HID), bf16),
            pltpu.VMEM((SEQ, D), bf16),
            pltpu.VMEM((SEQ, D), bf16),
            pltpu.VMEM((D, HID), bf16),
            pltpu.VMEM((HID, D), bf16),
            pltpu.VMEM((4, 16, D), bf16),
            pltpu.VMEM((TOK + 32, D), f32),
            pltpu.VMEM((WIDE, D), f32),
            pltpu.VMEM((WIDE, 128), f32),
            pltpu.VMEM((SEQ, HID), bf16),
            pltpu.VMEM((SEQ, HID), f32),
            pltpu.VMEM((SEQ, HID), bf16),
            pltpu.VMEM((SEQ + 16, D), f32),
            pltpu.VMEM((2, WIDE, D), bf16),
            pltpu.VMEM((2, WIDE, D), bf16),
            pltpu.VMEM((WIDE, D), bf16),
            pltpu.VMEM((WIDE, D), bf16),
            pltpu.VMEM((2, 4, XB, HID), bf16),
            pltpu.VMEM((2, 2, XB // 2, HID), bf16),
            pltpu.VMEM((2, 2, XB, HID), bf16),
            pltpu.VMEM((2, 4, YB, HID), bf16),
            pltpu.VMEM((2, 2, YB // 2, HID), bf16),
            pltpu.VMEM((2, 2, YB, HID), bf16),
            pltpu.VMEM((WIDE, D), f32),
            pltpu.VMEM((TOK, D), bf16),
            pltpu.VMEM((2, 8, D), f32),
            pltpu.VMEM((16, D), f32),
            pltpu.VMEM((16, D), f32),
            pltpu.VMEM((8, D), f32),
            pltpu.VMEM((8, D), f32),
            pltpu.VMEM((4, 8, D), f32),
            pltpu.VMEM((4, 8, D), f32),
            pltpu.VMEM((8, D), f32),
            pltpu.VMEM((1, HID), f32),
            pltpu.SemaphoreType.DMA((N_COPIES,)),
            pltpu.SemaphoreType.DMA((N_COPIES,)),
            pltpu.SemaphoreType.DMA((N_LOCAL,)),
        ],
        compiler_params=pltpu.CompilerParams(
            collective_id=0, has_side_effects=True, vmem_limit_bytes=56 * 1024 * 1024
        ),
    )(
        x_stash, h_stash, cotangent, plan, jnp.swapaxes(conv_w, 0, 1), conv_b, norm_gain, shift_b, w_in, w_out
    )
    gin, gwi, gwo, conv, affine, bias = pl.pallas_call(
        deliver,
        out_shape=(
            jax.ShapeDtypeStruct((1, TOK, D), bf16),
            jax.ShapeDtypeStruct((YB, HID), f32),
            jax.ShapeDtypeStruct((YB, HID), f32),
            jax.ShapeDtypeStruct((8, D), f32),
            jax.ShapeDtypeStruct((3, 1, D), f32),
            jax.ShapeDtypeStruct((1, 2 * D), f32),
        ),
        in_specs=[vmem] * 4,
        out_specs=(vmem,) * 6,
    )(*results)
    return (
        gin,
        gwi[None],
        gwo.T[None],
        conv[None],
        jnp.swapaxes(affine, 0, 1),
        bias,
    )


def solution(mesh):
    return jax.shard_map(
        per_device,
        mesh=mesh,
        in_specs=(
            P("pipe", None, ("dp", "tensor"), None),
            P("pipe", None, "dp", "tensor"),
            P("pipe", ("dp", "tensor"), None),
            P("pipe"),
            P("pipe", None, None),
            P("pipe", None),
            P("pipe", None),
            P("pipe", None),
            P("pipe", None, "tensor"),
            P("pipe", "tensor", None),
        ),
        out_specs=(
            P("pipe", ("dp", "tensor"), None),
            P("pipe", "dp", "tensor"),
            P("pipe", "tensor", "dp"),
            P("pipe", None, None),
            P("pipe", None, None),
            P("pipe", None),
        ),
        check_vma=False,
    )
```

```python
import math

import jax
import jax.numpy as jnp
from jax import lax
from jax.experimental import pallas as pl
from jax.experimental.pallas import tpu as pltpu
from jax.sharding import PartitionSpec as P

MESH = pl.DeviceIdType.MESH
f32 = jnp.float32
bf16 = jnp.bfloat16

gelu_coef = 0.044715
root_coef = math.sqrt(2.0 / math.pi)
norm_eps = 1e-06

D = 1536
HID = 768
SEQ = 512
TOK = 128
KER = 7
CH = 384
XB = D // 4
YB = XB // 4
WIDE = TOK + 16
N_COPIES = 112
CHUNKS = ((0, 256), (256, 512), (0, 512), (512, 256))
N_LOCAL = 16


def dot_tn(a, b):
    return lax.dot_general(a, b, (((0,), (0,)), ((), ())), preferred_element_type=f32)


def dot_nt(a, b):
    return lax.dot_general(a, b, (((1,), (1,)), ((), ())), preferred_element_type=f32)


def kernel(
    x_hbm, h_hbm, g_hbm, plan_ref, cw_hbm, cb_hbm, gain_hbm, shift_hbm, win_hbm, wout_hbm,
    gin_out, gwi_out, gwo_out, small_out, cw_ref, cb_ref, gain_ref, shift_ref,
    xs, hs, gf, sf, win, wout, halo, xw, normed, inv, active, slope, dh, dpart, s1, r1, s2, r2t,
    part, xr2, xrx, q, yr2, yrx, dmix, gx, accs, sm, arc, ar, arr, arx, ary, arf, bias, ssem, rsem, lsem,
):
    dp = lax.axis_index("dp")
    pz = lax.axis_index("pipe")
    t = lax.axis_index("tensor")
    xi, yi = dp // 4, dp % 4
    ylo, core = t // 2, t % 2
    npipe = lax.axis_size("pipe")

    def dev(dp_=None, pz_=None, t_=None):
        return (
            dp if dp_ is None else dp_,
            pz if pz_ is None else pz_,
            t if t_ is None else t_,
        )

    core_dev = dev(t_=ylo * 2 + 1 - core)
    chip_dev = dev(t_=(t + 2) % 4)
    diag_dev = dev(t_=(1 - ylo) * 2 + 1 - core)
    seq_next, seq_prev = dev(t_=(t + 1) % 4), dev(t_=(t + 3) % 4)
    xp, xm = dev(dp_=((xi + 1) % 4) * 4 + yi), dev(dp_=((xi + 3) % 4) * 4 + yi)
    yp, ym = dev(dp_=xi * 4 + (yi + 1) % 4), dev(dp_=xi * 4 + (yi + 3) % 4)
    x2 = dev(dp_=((xi + 2) % 4) * 4 + yi)
    y_a, y_b = dev(dp_=xi * 4 + yi + 1 - 2 * (yi % 2)), dev(dp_=xi * 4 + 3 - yi)
    z_down = dev(pz_=(pz + npipe - 1) % npipe)
    z_up = dev(pz_=(pz + 1) % npipe)

    used = [0, 0]
    sent = []

    def remote(src, dst, to):
        i = used[0]
        used[0] += 1
        assert i < N_COPIES
        copy = pltpu.make_async_remote_copy(
            src_ref=src, dst_ref=dst, send_sem=ssem.at[i], recv_sem=rsem.at[i],
            device_id=to, device_id_type=MESH,
        )
        copy.start()
        sent.append(copy)
        return copy

    def local(src, dst):
        i = used[1]
        used[1] += 1
        assert i < N_LOCAL
        copy = pltpu.make_async_copy(src, dst, lsem.at[i])
        copy.start()
        return copy

    own_rows = pl.ds(pl.multiple_of(t * TOK, TOK), TOK)

    barrier = pltpu.get_barrier_semaphore()
    for to in (core_dev, chip_dev, diag_dev, xp, xm, x2, yp, ym, z_down, z_up):
        pl.semaphore_signal(barrier, inc=1, device_id=to, device_id_type=MESH)
    lx = local(x_hbm.at[0], xs)
    lh = local(h_hbm.at[0], hs)
    pl.semaphore_wait(barrier, 10)

    def block_cols(k):
        return pl.ds(pl.multiple_of(((xi + k) % 4) * XB, XB), XB)

    order = (2, 1, 3, 0)
    chip_rows = pl.ds(pl.multiple_of(((t + 2) % 4) * TOK, TOK), TOK)

    def pass_on(copies, full, k):
        copies[k].wait_recv()
        chip_block = full.at[chip_rows, block_cols(k)]
        return remote(chip_block, chip_block, core_dev)

    def send_g(k, to):
        return remote(g_hbm.at[0, :, block_cols(k)], gf.at[own_rows, block_cols(k)], to)

    g_chip = {2: send_g(2, chip_dev)}
    slot = plan_ref[0]
    lx.wait()
    halo[0] = xs[slot, TOK - 16 :, :]
    halo[1] = xs[slot, :16, :]
    h_next = remote(halo.at[0], halo.at[2], seq_next)
    h_prev = remote(halo.at[1], halo.at[3], seq_prev)
    for k in order[1:]:
        g_chip[k] = send_g(k, chip_dev)
    g_core = {k: send_g(k, core_dev) for k in order}
    small_loads = [
        local(cw_hbm, cw_ref), local(cb_hbm, cb_ref), local(gain_hbm, gain_ref), local(shift_hbm, shift_ref)
    ]
    lg = local(g_hbm.at[0], gf.at[own_rows])
    lwo = local(wout_hbm.at[0], wout)
    lwi = local(win_hbm.at[0], win)

    def widen(i, carry):
        rows = pl.ds(pl.multiple_of(i * 16, 16), 16)
        xw[pl.ds(pl.multiple_of(16 + i * 16, 16), 16), :] = xs[slot, rows, :].astype(f32)
        return carry

    lax.fori_loop(0, TOK // 16, widen, 0)

    lh.wait()

    def gelu_rows(i, carry):
        rows = pl.ds(pl.multiple_of(i * 16, 16), 16)
        hv = hs[slot, rows, :].astype(f32)
        square = hv * hv
        tangent = jnp.tanh(root_coef * hv * (1.0 + gelu_coef * square))
        half = 0.5 + 0.5 * tangent
        value = hv * half
        active[rows, :] = value.astype(bf16)
        slope[rows, :] = half + value * (1.0 - tangent) * (
            root_coef + (3.0 * gelu_coef * root_coef) * square
        )
        return carry

    lax.fori_loop(0, SEQ // 16, gelu_rows, 0)

    for copy in small_loads:
        copy.wait()
    h_next.wait_recv()
    h_prev.wait_recv()
    xw[0:16, :] = jnp.where(t > 0, halo[2].astype(f32), 0.0)
    xw[16 + TOK : 32 + TOK, :] = jnp.where(t < 3, halo[3].astype(f32), 0.0)

    def norm_rows(first, count):
        near = xw[pl.ds(first, count + 16), :]
        out = cb_ref[...] + cw_ref[0] * near[5 : 5 + count]
        for k in range(1, KER):
            out = out + cw_ref[k] * near[5 + k : 5 + k + count]
        center = out - jnp.mean(out, -1, keepdims=True)
        istd = lax.rsqrt(jnp.mean(center * center, -1, keepdims=True) + norm_eps)
        return center * istd, istd

    def own_norm(i, carry):
        rows = pl.ds(pl.multiple_of(i * 16, 16), 16)
        value, istd = norm_rows(pl.multiple_of(16 * i + 8, 8), 16)
        normed[rows, :] = value
        inv[rows, :] = jnp.broadcast_to(istd, (16, 128))
        sf[pl.ds(pl.multiple_of(t * TOK + i * 16, 16), 16), :] = (
            value * gain_ref[...] + shift_ref[...]
        ).astype(bf16)
        return carry

    lax.fori_loop(0, TOK // 32, own_norm, 0)
    g_pass = {2: pass_on(g_chip, gf, 2)}
    lax.fori_loop(TOK // 32, TOK // 16, own_norm, 0)

    def send_s(k, to):
        own_block = sf.at[own_rows, block_cols(k)]
        return remote(own_block, own_block, to)

    s_chip = {k: send_s(k, chip_dev) for k in order}
    s_core = {k: send_s(k, core_dev) for k in order}
    def hidden_grads(half):
        base = pl.multiple_of(half * 256, 256)
        for j in range(2):
            cols = pl.ds(j * CH, CH)
            d = dot_nt(gf[pl.ds(base, 256), :], wout[j * CH : (j + 1) * CH, :])
            d = d * slope[pl.ds(base, 256), cols]
            bias[:, cols] += jnp.sum(d, 0, keepdims=True)
            dh[pl.ds(base, 256), cols] = d.astype(bf16)

    def part_scaled(half):
        base = pl.multiple_of(half * 256, 256)

        def block(j, carry):
            cols = pl.ds(pl.multiple_of(j * CH, CH), CH)
            dpart[pl.ds(pl.multiple_of(base + 8, 8), 256), cols] = dot_nt(
                dh[pl.ds(base, 256), :], win[cols, :]
            )
            return carry

        lax.fori_loop(0, D // CH, block, 0)

    def weight_part(m, k, src, hidden):
        part[m, k] = dot_tn(src[:, block_cols(k)], hidden[...]).astype(bf16)

    def ring_far(own, two, half, cols, plus, minus):
        far_a = remote(own.at[2, pl.ds(0, half), cols], two.at[0, :, cols], plus)
        far_b = remote(own.at[2, pl.ds(half, half), cols], two.at[1, :, cols], minus)
        return far_a, far_b

    def ring_near(own, last, half, cols, plus, minus):
        low, high = pl.ds(0, half), pl.ds(half, half)
        near_b = remote(own.at[1, high, cols], last.at[0, high, cols], plus)
        near_a = remote(own.at[3, low, cols], last.at[1, low, cols], minus)
        return near_a, near_b

    def ring_second(copies, own, two, last, half, cols, plus, minus):
        far_a, far_b, near_a, near_b = copies
        low, high = pl.ds(0, half), pl.ds(half, half)
        far_a.wait_recv()

        def add_a(i, carry):
            rows = pl.ds(pl.multiple_of(i * 48, 16), 48)
            own[1, rows, cols] = (
                own[1, rows, cols].astype(f32) + two[0, rows, cols].astype(f32)
            ).astype(bf16)
            return carry

        lax.fori_loop(0, half // 48, add_a, 0)
        sum_a = remote(own.at[1, low, cols], last.at[0, low, cols], plus)
        far_b.wait_recv()

        def add_b(i, carry):
            rows = pl.ds(pl.multiple_of(half + i * 48, 16), 48)
            here = pl.ds(pl.multiple_of(i * 48, 16), 48)
            own[3, rows, cols] = (
                own[3, rows, cols].astype(f32) + two[1, here, cols].astype(f32)
            ).astype(bf16)
            return carry

        lax.fori_loop(0, half // 48, add_b, 0)
        sum_b = remote(own.at[3, high, cols], last.at[1, high, cols], minus)
        return near_a, near_b, sum_a, sum_b

    x_copies, y_copies = {}, {}

    def chunk(c):
        return c // 2, pl.ds(*CHUNKS[c])

    def x_far(c):
        m, cols = chunk(c)
        x_copies[c] = ring_far(part.at[m], xr2.at[m], XB // 2, cols, xp, xm)

    def x_near(c):
        m, cols = chunk(c)
        x_copies[c] += ring_near(part.at[m], xrx.at[m], XB // 2, cols, xp, xm)

    def x_second(c):
        m, cols = chunk(c)
        x_copies[c] = ring_second(
            x_copies[c], part.at[m], xr2.at[m], xrx.at[m], XB // 2, cols, xp, xm
        )

    def x_third(c):
        m, cols = chunk(c)
        for copy in x_copies[c]:
            copy.wait_recv()

        def block(k, carry):
            for piece in range(2):
                rows = pl.ds(pl.multiple_of(((yi + k) % 4) * YB + piece * 48, 16), 48)
                q[m, k, pl.ds(piece * 48, 48), cols] = (
                    part[m, 0, rows, cols].astype(f32)
                    + xrx[m, 0, rows, cols].astype(f32)
                    + xrx[m, 1, rows, cols].astype(f32)
                ).astype(bf16)
            return carry

        lax.fori_loop(0, 4, block, 0)

    def y_first(c):
        m, cols = chunk(c)
        y_copies[c] = ring_far(q.at[m], yr2.at[m], YB // 2, cols, yp, ym)
        y_copies[c] += ring_near(q.at[m], yrx.at[m], YB // 2, cols, yp, ym)

    def y_second(c):
        m, cols = chunk(c)
        y_copies[c] = ring_second(
            y_copies[c], q.at[m], yr2.at[m], yrx.at[m], YB // 2, cols, yp, ym
        )

    def y_third(c):
        m, cols = chunk(c)
        for copy in y_copies[c]:
            copy.wait_recv()
        out = (gwo_out, gwi_out)[m]
        for piece in range(2):
            rows = pl.ds(piece * 48, 48)
            out[rows, cols] = (
                q[m, 0, rows, cols].astype(f32)
                + yrx[m, 0, rows, cols].astype(f32)
                + yrx[m, 1, rows, cols].astype(f32)
            )

    lg.wait()
    for k in order:
        g_core[k].wait_recv()
    g_pass[2].wait_recv()
    weight_part(0, 2, gf, active)
    x_far(0)
    x_far(1)

    for first, row in ((0, TOK), (TOK + 8, TOK + 8)):
        value, istd = norm_rows(first, 8)
        normed[row : row + 8, :] = value
        inv[row : row + 8, :] = jnp.broadcast_to(istd, (8, 128))

    bias[...] = jnp.zeros_like(bias)
    dpart[0:8, :] = jnp.zeros((8, D), f32)
    dpart[SEQ + 8 : SEQ + 16, :] = jnp.zeros((8, D), f32)
    lwo.wait()
    hidden_grads(ylo)
    g_pass[1] = pass_on(g_chip, gf, 1)
    lwi.wait()
    part_scaled(ylo)

    g_pass[3] = pass_on(g_chip, gf, 3)
    g_pass[1].wait_recv()
    weight_part(0, 1, gf, active)
    g_pass[0] = pass_on(g_chip, gf, 0)
    g_pass[3].wait_recv()
    weight_part(0, 3, gf, active)
    x_near(0)
    g_pass[0].wait_recv()
    hidden_grads(1 - ylo)
    part_scaled(1 - ylo)

    def target_rows(tt, i):
        return dpart[pl.ds(pl.multiple_of(8 + tt * TOK + i * 16, 8), 16), :]

    def target_rim(tt, after):
        return dpart[pl.ds(pl.multiple_of(tt * TOK + after * (TOK + 8), 8), 8), :]

    core_far = (1 - ylo) * 2 + 1 - core
    core_near = ylo * 2 + 1 - core
    core_sums = []
    for n, tt in enumerate((core_far, core_near)):

        def fill(i, carry, n=n, tt=tt):
            s1[n, pl.ds(pl.multiple_of(i * 16, 16), 16), :] = target_rows(tt, i).astype(bf16)
            return carry

        lax.fori_loop(0, TOK // 16, fill, 0)
        s1[n, TOK:, :] = jnp.concatenate([target_rim(tt, 0), target_rim(tt, 1)], 0).astype(bf16)
        core_sums.append(remote(s1.at[n], r1.at[n], core_dev))

    weight_part(0, 0, gf, active)
    x_second(0)
    x_near(1)

    core_sums[0].wait_recv()
    chip_t = (t + 2) % 4

    def add_far(i, carry):
        rows = pl.ds(pl.multiple_of(i * 16, 16), 16)
        s2[rows, :] = (target_rows(chip_t, i) + r1[0, rows, :].astype(f32)).astype(bf16)
        return carry

    lax.fori_loop(0, TOK // 16, add_far, 0)
    s2[TOK:, :] = (
        jnp.concatenate([target_rim(chip_t, 0), target_rim(chip_t, 1)], 0) + r1[0, TOK:, :].astype(f32)
    ).astype(bf16)
    far_sum = remote(s2, r2t, chip_dev)

    x_second(1)
    s_pass = {2: pass_on(s_chip, sf, 2)}
    for k in order:
        s_core[k].wait_recv()
    s_pass[2].wait_recv()
    weight_part(1, 2, sf, dh)
    x_far(2)
    for k in order[1:]:
        s_pass[k] = pass_on(s_chip, sf, k)
    s_pass[1].wait_recv()
    weight_part(1, 1, sf, dh)
    s_pass[3].wait_recv()
    weight_part(1, 3, sf, dh)
    x_near(2)
    x_far(3)
    s_pass[0].wait_recv()
    weight_part(1, 0, sf, dh)
    x_third(0)
    y_first(0)

    core_sums[1].wait_recv()
    far_sum.wait_recv()
    accs[...] = jnp.zeros_like(accs)

    def norm_back(ds, rows, count):
        nv = normed[rows, :]
        dn = ds * gain_ref[...]
        mean_d = jnp.mean(dn, -1, keepdims=True)
        mean_p = jnp.mean(dn * nv, -1, keepdims=True)
        return nv, inv[rows, 0:1] * (dn - mean_d - nv * mean_p)

    def own_back(i, carry):
        rows = pl.ds(pl.multiple_of(i * 16, 16), 16)
        ds = target_rows(t, i) + r1[1, rows, :].astype(f32) + r2t[rows, :].astype(f32)
        nv, dm = norm_back(ds, rows, 16)
        dmix[pl.ds(pl.multiple_of(8 + i * 16, 8), 16), :] = dm
        dsn = ds * nv
        accs[0] += dsn[0:8] + dsn[8:16]
        accs[1] += ds[0:8] + ds[8:16]
        return carry

    lax.fori_loop(0, TOK // 16, own_back, 0)
    rim = pl.ds(TOK, 16)
    rim_ds = (
        jnp.concatenate([target_rim(t, 0), target_rim(t, 1)], 0)
        + r1[1, TOK:, :].astype(f32)
        + r2t[TOK:, :].astype(f32)
    )
    _, rim_dm = norm_back(rim_ds, rim, 16)
    dmix[0:8, :] = rim_dm[0:8]
    dmix[TOK + 8 : TOK + 16, :] = rim_dm[8:16]


    def input_rows(i, carry):
        near = dmix[pl.ds(pl.multiple_of(16 * i, 16), 32), :]
        d = cw_ref[0] * near[11:27]
        for k in range(1, KER):
            d = d + cw_ref[k] * near[11 - k : 27 - k]
        gv = gf[pl.ds(pl.multiple_of(t * TOK + i * 16, 16), 16), :].astype(f32)
        gx[pl.ds(pl.multiple_of(i * 16, 16), 16), :] = jnp.where(pz > 0, gv + d, 0.0).astype(bf16)
        return carry

    z_copies = []
    for piece in range(2):
        lax.fori_loop(piece * 4, piece * 4 + 4, input_rows, 0)
        rows = pl.ds(piece * 64, 64)
        z_copies.append(remote(gx.at[rows], gin_out.at[0, rows], z_down))

    sm[...] = jnp.zeros_like(sm)

    def tap_sums(j, carry):
        cols = pl.ds(pl.multiple_of(j * 256, 256), 256)

        def rows_step(i, totals):
            dm = dmix[pl.ds(pl.multiple_of(8 + 8 * i, 8), 8), cols]
            near = xw[pl.ds(pl.multiple_of(8 + 8 * i, 8), 24), cols]
            out = [totals[k] + dm * near[5 + k : 13 + k] for k in range(KER)]
            out.append(totals[KER] + dm)
            return tuple(out)

        totals = lax.fori_loop(
            0, TOK // 8, rows_step, tuple(jnp.zeros((8, 256), f32) for _ in range(KER + 1))
        )
        for k in range(KER + 1):
            sm[k : k + 1, cols] = jnp.sum(totals[k], 0, keepdims=True)

        def g_step(i, total):
            gv = gf[pl.ds(pl.multiple_of(t * TOK + i * 16, 16), 16), cols].astype(f32)
            return total + gv[0:8] + gv[8:16]

        total = lax.fori_loop(0, TOK // 16, g_step, jnp.zeros((8, 256), f32))
        sm[10:11, cols] = jnp.sum(total, 0, keepdims=True)
        sm[8:9, cols] = jnp.sum(accs[0, :, cols], 0, keepdims=True)
        sm[9:10, cols] = jnp.sum(accs[1, :, cols], 0, keepdims=True)
        return carry

    lax.fori_loop(0, D // 256, tap_sums, 0)
    zero_row = jnp.zeros((1, HID), f32)
    for s in range(4):
        sm[11 + s // 2 : 12 + s // 2, (s % 2) * HID : (s % 2 + 1) * HID] = jnp.where(
            t == s, bias[...], zero_row
        )
    a_core = remote(sm, arc, core_dev)

    x_second(2)
    x_near(3)
    a_core.wait_recv()
    my8 = pl.ds(pl.multiple_of(core * 8, 8), 8)
    ar[...] = sm[my8, :] + arc[my8, :]
    a_chip = remote(ar, arr, chip_dev)
    x_third(1)
    y_first(1)
    y_second(0)
    x_second(3)
    a_chip.wait_recv()
    arx[xi] = ar[...] + arr[...]
    a_x = [remote(arx.at[xi], arx.at[xi], to) for to in (xp, xm, x2)]
    y_third(0)
    y_second(1)
    x_third(2)
    y_first(2)
    for copy in a_x:
        copy.wait_recv()
    ary[0] = (arx[0] + arx[1]) + (arx[2] + arx[3])
    a_y = remote(ary.at[0], ary.at[1], y_a)
    y_third(1)
    y_second(2)
    a_y.wait_recv()
    ary[2] = ary[0] + ary[1]
    a_y = remote(ary.at[2], ary.at[3], y_b)
    x_third(3)
    y_first(3)
    y_third(2)
    a_y.wait_recv()
    arf[...] = ary[2] + ary[3]
    small_out[my8, :] = arf[...]
    a_back = remote(arf, small_out.at[my8], core_dev)
    y_second(3)
    y_third(3)
    a_back.wait_recv()
    for copy in z_copies:
        copy.wait_recv()
    for copy in sent:
        copy.wait_send()


def deliver(gin, gwi, gwo, small, gin_out, gwi_out, gwo_out, conv_out, affine_out, bias_out):
    gin_out[...] = gin[...]
    gwi_out[...] = gwi[...]
    gwo_out[...] = gwo[...]
    conv_out[...] = small[0:8, :]
    for i in range(3):
        affine_out[i] = small[8 + i : 9 + i, :]
    for i in range(2):
        bias_out[:, i * D : (i + 1) * D] = small[11 + i : 12 + i, :]


def per_device(x_stash, h_stash, cotangent, plan, conv_w, conv_b, norm_gain, shift_b, w_in, w_out):
    anyspace = pl.BlockSpec(memory_space=pl.ANY)
    vmem = pl.BlockSpec(memory_space=pltpu.VMEM)
    smem = pl.BlockSpec(memory_space=pltpu.SMEM)
    results = pl.pallas_call(
        kernel,
        out_shape=(
            jax.ShapeDtypeStruct((1, TOK, D), bf16),
            jax.ShapeDtypeStruct((YB, HID), f32),
            jax.ShapeDtypeStruct((YB, HID), f32),
            jax.ShapeDtypeStruct((16, D), f32),
        ),
        in_specs=[anyspace, anyspace, anyspace, smem] + [anyspace] * 6,
        out_specs=(anyspace, vmem, vmem, vmem),
        scratch_shapes=[
            pltpu.VMEM((KER, 1, D), f32),
            pltpu.VMEM((1, D), f32),
            pltpu.VMEM((1, D), f32),
            pltpu.VMEM((1, D), f32),
            pltpu.VMEM((2, TOK, D), bf16),
            pltpu.VMEM((2, SEQ, HID), bf16),
            pltpu.VMEM((SEQ, D), bf16),
            pltpu.VMEM((SEQ, D), bf16),
            pltpu.VMEM((D, HID), bf16),
            pltpu.VMEM((HID, D), bf16),
            pltpu.VMEM((4, 16, D), bf16),
            pltpu.VMEM((TOK + 32, D), f32),
            pltpu.VMEM((WIDE, D), f32),
            pltpu.VMEM((WIDE, 128), f32),
            pltpu.VMEM((SEQ, HID), bf16),
            pltpu.VMEM((SEQ, HID), f32),
            pltpu.VMEM((SEQ, HID), bf16),
            pltpu.VMEM((SEQ + 16, D), f32),
            pltpu.VMEM((2, WIDE, D), bf16),
            pltpu.VMEM((2, WIDE, D), bf16),
            pltpu.VMEM((WIDE, D), bf16),
            pltpu.VMEM((WIDE, D), bf16),
            pltpu.VMEM((2, 4, XB, HID), bf16),
            pltpu.VMEM((2, 2, XB // 2, HID), bf16),
            pltpu.VMEM((2, 2, XB, HID), bf16),
            pltpu.VMEM((2, 4, YB, HID), bf16),
            pltpu.VMEM((2, 2, YB // 2, HID), bf16),
            pltpu.VMEM((2, 2, YB, HID), bf16),
            pltpu.VMEM((WIDE, D), f32),
            pltpu.VMEM((TOK, D), bf16),
            pltpu.VMEM((2, 8, D), f32),
            pltpu.VMEM((16, D), f32),
            pltpu.VMEM((16, D), f32),
            pltpu.VMEM((8, D), f32),
            pltpu.VMEM((8, D), f32),
            pltpu.VMEM((4, 8, D), f32),
            pltpu.VMEM((4, 8, D), f32),
            pltpu.VMEM((8, D), f32),
            pltpu.VMEM((1, HID), f32),
            pltpu.SemaphoreType.DMA((N_COPIES,)),
            pltpu.SemaphoreType.DMA((N_COPIES,)),
            pltpu.SemaphoreType.DMA((N_LOCAL,)),
        ],
        compiler_params=pltpu.CompilerParams(
            collective_id=0, has_side_effects=True, vmem_limit_bytes=56 * 1024 * 1024
        ),
    )(
        x_stash, h_stash, cotangent, plan, jnp.swapaxes(conv_w, 0, 1), conv_b, norm_gain, shift_b, w_in, w_out
    )
    gin, gwi, gwo, conv, affine, bias = pl.pallas_call(
        deliver,
        out_shape=(
            jax.ShapeDtypeStruct((1, TOK, D), bf16),
            jax.ShapeDtypeStruct((YB, HID), f32),
            jax.ShapeDtypeStruct((YB, HID), f32),
            jax.ShapeDtypeStruct((8, D), f32),
            jax.ShapeDtypeStruct((3, 1, D), f32),
            jax.ShapeDtypeStruct((1, 2 * D), f32),
        ),
        in_specs=[vmem] * 4,
        out_specs=(vmem,) * 6,
    )(*results)
    return (
        gin,
        gwi[None],
        gwo.T[None],
        conv[None],
        jnp.swapaxes(affine, 0, 1),
        bias,
    )


def solution(mesh):
    return jax.shard_map(
        per_device,
        mesh=mesh,
        in_specs=(
            P("pipe", None, ("dp", "tensor"), None),
            P("pipe", None, "dp", "tensor"),
            P("pipe", ("dp", "tensor"), None),
            P("pipe"),
            P("pipe", None, None),
            P("pipe", None),
            P("pipe", None),
            P("pipe", None),
            P("pipe", None, "tensor"),
            P("pipe", "tensor", None),
        ),
        out_specs=(
            P("pipe", ("dp", "tensor"), None),
            P("pipe", "dp", "tensor"),
            P("pipe", "tensor", "dp"),
            P("pipe", None, None),
            P("pipe", None, None),
            P("pipe", None),
        ),
        check_vma=False,
    )
```
